128 devices in a mesh: tm: 8 (over z, core), chan: 16 (over x, y).
Axes of the slice: x: 4, y: 4, z: 4, core: 2. Of those that a mesh axis runs over, the one named last changes fastest.
Arguments:
- records: float32 [2048, 32768], P(None, ('tm', 'chan')), may hold values from -6 to 6
- pairs: int32 [48, 2], replicated, may hold values from 0 to 15, as said below
- owners: int32 [48, 1], replicated, may hold values from 0 to 15; in each aligned block of 48 rows (0 to 47, 48 to 95, ...) at most 6 rows name the same one
- starts: int32 [58], replicated, may hold values from 0 to 31744, as said below
Outputs:
- cross_spectra: bfloat16 [96, 384, 2, 128, 128], P('chan', 'tm')
The draws below stay inside these ranges and needn't reach their ends.
Inputs may be any that keep to these rules, and one draw needn't show every extreme that they name: `pairs`: each row holds blocks a, b with 0 <= b - a <= 2; every block is the first member of exactly 3 rows. `owners`: no owner holds more than 6 pairs and some owner holds exactly 6; every owner holds at least one. `starts`: the first possible start 0 and the last possible start 32768 - 1024 each occur.
All inputs are finite; a program needn't handle non-finite values.
Results may differ from the reference program's by a relative error of at most 0.0049.
Values may be sent and summed in bfloat16 or wider, within the bound.
A program may use at most 256 MiB of HBM per device.

```python
import math
import jax
import jax.numpy as jnp
import numpy as np
from jax import lax

BLOCK = 128
NFFT = 1024
NFREQ = 384
WBAND = 64
SEG = 58
PAIR_DEV = 3
PMAX = 6
NBLOCKS = 16
CHANNELS = 2048
SAMPLES = 32768
NPAIR = 48
N_CHAN = 16


def draw_pairs(key, part):
    key = jax.random.fold_in(key, 11)
    key_order, key_step = jax.random.split(key)
    first = jnp.tile(jax.random.permutation(key_order, NBLOCKS), PAIR_DEV)
    offset = jax.random.randint(key_step, (NPAIR,), 0, 3)
    second = jnp.minimum(first + offset, NBLOCKS - 1)
    return jnp.stack([first, second], axis=1).astype(jnp.int32)


def draw_starts(key, part):
    key = jax.random.fold_in(key, 23)
    key_vals, key_high, key_low = jax.random.split(key, 3)
    top = SAMPLES - NFFT
    values = jax.random.randint(key_vals, (SEG,), 0, top + 1)
    high = jax.random.randint(key_high, (), 0, SEG)
    low = (high + jax.random.randint(key_low, (), 1, SEG)) % SEG
    values = values.at[high].set(top).at[low].set(0)
    return values.astype(jnp.int32)


def shard_levels(own_key, shape, cuts, low, top_value):
    loudness, own = 1.0, jax.random.fold_in(own_key, 6)
    for axis_at, shards_of in cuts:
        steps = jnp.exp(jax.random.uniform(jax.random.fold_in(own, axis_at), (shards_of,), jnp.float32, low / len(cuts), top_value / len(cuts)))
        loudness = loudness * jnp.repeat(steps, shape[axis_at] // shards_of).reshape([-1 if axis == axis_at else 1 for axis in range(len(shape))])
    return loudness


def shared_out(stream_key, own, number, rows, count, top, limit, lean):
    order = jax.random.permutation(stream_key, count)
    packed, common = load_shares(count, rows * top, limit, lean, True), load_shares(count, rows * top, limit, lean, False)
    places = jnp.arange(count)

    def named(sizes, turn):
        used = int((sizes > 0).sum())
        fixed = max(1, used // 4)
        passed = fixed + (places - fixed + turn * (used - fixed)) % max(1, count - fixed)
        return jnp.zeros((count,), jnp.int32).at[order[jnp.where(places < fixed, places, passed)]].set(jnp.asarray(sizes, jnp.int32))

    sizes = jnp.where(number % 4 == 0, named(packed, number // 4), named(common, number - number // 4 - 1))
    mixed = jax.random.permutation(jax.random.fold_in(own, 3), count)
    source_of, sink = mixed[0:count // 2 * 2:2], mixed[1:count // 2 * 2:2]
    slack = jnp.minimum(sizes[source_of] - 1, limit - sizes[sink]) // 2
    slack = jnp.where((source_of == order[0]) | (sink == order[0]) | (sizes[sink] == 0), 0, jnp.maximum(slack, 0))
    passed = jax.random.randint(jax.random.fold_in(own, 4), (count // 2,), 0, 1 << 20) % (slack + 1)
    sizes = sizes.at[source_of].add(-passed).at[sink].add(passed)
    items = jnp.searchsorted(jnp.cumsum(sizes), jnp.arange(rows * top), side="right").astype(jnp.int32)
    grid = items.reshape(top, rows).T
    grid = grid[jax.random.permutation(jax.random.fold_in(own, 1), rows)]
    turn = jax.random.randint(jax.random.fold_in(own, 2), (rows, 1), 0, top)
    return jnp.take_along_axis(grid, (jnp.arange(top)[None, :] + turn) % top, axis=1)


def load_shares(count, total, most, skew, full):
    loads = [(1 << 20) // math.isqrt(standing ** skew) + 1 for standing in range(1, count + 1)]
    largest = most if full else min(most, max(-(-total // count), total * loads[0] // sum(loads)))
    least = 1 if total - largest >= count - 1 else 0
    counts, rest = [largest] + [least] * (count - 1), total - largest - least * (count - 1)
    while rest > 0:
        candidates = [i for i in range(1, count) if counts[i] < largest] or [i for i in range(1, count) if counts[i] < most]
        whole, remaining = sum([loads[i] for i in candidates]), rest
        for i in candidates:
            more = min(most - counts[i], max(1, remaining * loads[i] // whole), rest)
            counts[i] = counts[i] + more
            rest = rest - more
    return np.array(counts)


def centred(stream_key, extent, deviation, bound, shards=(), held_as=jnp.bfloat16):
    result = jax.random.normal(stream_key, extent, jnp.float32) * deviation
    if len(shards) > 0:
        result = shard_levels(stream_key, extent, shards, -0.22, 0.18) * result
    return jnp.clip(result, min=-bound, max=bound).astype(held_as)


def setup_inputs(seed: int = 0) -> dict:
    seeds = jax.random.split(jax.random.key(seed), 5)
    records = centred(seeds[0], (CHANNELS, SAMPLES), 1.0, 6.0, ((1, 128),), jnp.float32)
    pairs = draw_pairs(jax.random.fold_in(seeds[4], 71), 0)
    owners_keys = jax.random.split(jax.random.fold_in(seeds[2], 1), NPAIR // NPAIR)
    owners_turns = jax.random.permutation(jax.random.fold_in(seeds[2], 3), NPAIR // NPAIR)
    owners = jax.vmap(lambda own, number: shared_out(jax.random.fold_in(seeds[2], 2), own, number, NPAIR, N_CHAN, 1, PMAX, 2))(owners_keys, owners_turns).reshape((NPAIR, 1))
    starts = draw_starts(jax.random.fold_in(seeds[4], 71), 0)
    return dict(records=records, pairs=pairs, owners=owners, starts=starts)


def slot_table(pairs, owners):
    owner = owners[:, 0]
    npair = owner.shape[0]
    order = jnp.arange(npair, dtype=jnp.int32)
    same = owner[:, None] == owner[None, :]
    before = order[None, :] < order[:, None]
    rank = lax.optimization_barrier(jnp.sum((same & before).astype(jnp.int32), axis=1))
    target = owner * PMAX + rank
    rows = jnp.arange(N_CHAN * PMAX, dtype=jnp.int32)
    match = target[None, :] == rows[:, None]
    live = jnp.any(match, axis=1)
    pair_id = lax.optimization_barrier(jnp.sum(jnp.where(match, order[None, :], 0), axis=1)).astype(jnp.int32)
    return (pairs[pair_id, 0], pairs[pair_id, 1], live)

def reference(records, pairs, owners, starts):

    def cut(begin):
        return lax.dynamic_slice_in_dim(records, begin, NFFT, 1)
    frames = jax.vmap(cut)(starts)
    steps_n = jnp.arange(NFFT).astype(jnp.float32)
    window = 0.5 - 0.5 * jnp.cos(2.0 * jnp.pi * steps_n / NFFT)
    spectrum = jnp.fft.rfft(frames * window, axis=-1)[..., :NFREQ]
    real_part = jnp.real(spectrum).astype(jnp.float32)
    imag_part = jnp.imag(spectrum).astype(jnp.float32)
    power = real_part * real_part + imag_part * imag_part
    seg_count, chans = (power.shape[0], power.shape[1])
    band = lax.optimization_barrier(jnp.mean(power.reshape(seg_count, chans, NFREQ // WBAND, WBAND), axis=-1, keepdims=True))
    scale = 1.0 / jnp.sqrt(band + 1e-06)
    white_re = (real_part.reshape(seg_count, chans, NFREQ // WBAND, WBAND) * scale).reshape(seg_count, chans, NFREQ).astype(jnp.bfloat16)
    white_im = (imag_part.reshape(seg_count, chans, NFREQ // WBAND, WBAND) * scale).reshape(seg_count, chans, NFREQ).astype(jnp.bfloat16)
    first, second, live = slot_table(pairs, owners)
    norm = 1.0 / math.sqrt(SEG)

    def one_slot(args):
        left, right, alive = args
        left_re = lax.dynamic_slice_in_dim(white_re, (left * BLOCK).astype(jnp.int32), BLOCK, 1).astype(jnp.float32)
        left_im = lax.dynamic_slice_in_dim(white_im, (left * BLOCK).astype(jnp.int32), BLOCK, 1).astype(jnp.float32)
        right_re = lax.dynamic_slice_in_dim(white_re, (right * BLOCK).astype(jnp.int32), BLOCK, 1).astype(jnp.float32)
        right_im = lax.dynamic_slice_in_dim(white_im, (right * BLOCK).astype(jnp.int32), BLOCK, 1).astype(jnp.float32)
        real_sum = jnp.einsum('sif,sjf->fij', left_re, right_re) + jnp.einsum('sif,sjf->fij', left_im, right_im)
        imag_sum = jnp.einsum('sif,sjf->fij', left_im, right_re) - jnp.einsum('sif,sjf->fij', left_re, right_im)
        stacked = jnp.stack([real_sum, imag_sum], axis=1) * norm
        stacked = jnp.where(alive, stacked, jnp.zeros_like(stacked))
        return stacked.astype(jnp.bfloat16)
    return lax.map(one_slot, (first, second, live))
```

```python
import functools
import math
import jax
import jax.numpy as jnp
import ml_dtypes
import numpy as np
from jax import lax
from jax.experimental import pallas as pl
from jax.experimental.pallas import tpu as pltpu
from jax.sharding import PartitionSpec as P

NFFT = 1024
NFREQ = 384
WBAND = 64
SEG = 58
SEGP = 64
PMAX = 6
LANES = 128
KROWS = 2 * SEG
QUAD = 4
VMEM_LIMIT = 56 * 1024 * 1024


def windowed_table():
    sample = np.arange(NFFT)
    freq = np.arange(NFREQ)
    angle = 2.0 * np.pi * ((freq[:, None] * sample[None, :]) % NFFT) / NFFT
    window = 0.5 - 0.5 * np.cos(2.0 * np.pi * sample / NFFT)
    table = np.concatenate([np.cos(angle), -np.sin(angle)], axis=0) * window[None, :]
    high = table.astype(np.float32).astype(ml_dtypes.bfloat16)
    low = (table - high.astype(np.float64)).astype(np.float32).astype(ml_dtypes.bfloat16)
    return high, low


def pick_table():
    pick = np.zeros((QUAD * KROWS, QUAD * LANES), np.float32)
    for q in range(QUAD):
        for part in range(2):
            for s in range(SEG):
                pick[q * KROWS + part * SEG + s, q * LANES + part * SEGP + s] = 1.0
    return pick.astype(ml_dtypes.bfloat16)


def slot_table(owners, owner_count):
    owner = owners[:, 0]
    npair = owner.shape[0]
    order = jnp.arange(npair, dtype=jnp.int32)
    same = owner[:, None] == owner[None, :]
    before = order[None, :] < order[:, None]
    rank = jnp.sum((same & before).astype(jnp.int32), axis=1)
    target = owner * PMAX + rank
    rows = jnp.arange(owner_count * PMAX, dtype=jnp.int32)
    match = target[None, :] == rows[:, None]
    live = jnp.any(match, axis=1)
    pair_id = jnp.sum(jnp.where(match, order[None, :], 0), axis=1)
    return (pair_id, live)


def spectra_kernel(chan_count, tm_count, starts_ref, rec_ref, high_ref, low_ref, out_ref, frames, spread):
    sub = rec_ref.shape[1]
    tiles = rec_ref.shape[2] // LANES
    total_tiles = rec_ref.shape[0] * tiles
    width = NFFT // LANES
    lane = lax.broadcasted_iota(jnp.int32, (sub, LANES), 1)
    for c in range(sub):
        frames[:, c * SEGP + SEG : (c + 1) * SEGP, :] = jnp.zeros(
            (width, SEGP - SEG, LANES), jnp.float32
        )

    def cut(s, carry):
        begin = starts_ref[s]
        base = jnp.minimum(begin // LANES, total_tiles - width - 1)
        over = begin - base * LANES
        shift = (LANES - over) % LANES
        turned = []
        for j in range(width + 1):
            tile = base + j
            piece = tile // tiles
            source = (piece % chan_count) * tm_count + piece // chan_count
            at = pl.multiple_of((tile % tiles) * LANES, LANES)
            turned.append(pltpu.roll(rec_ref[source, :, pl.ds(at, LANES)], shift, 1))
        keep = lane < LANES - over
        for j in range(width):
            frames[j, pl.ds(s, sub, stride=SEGP), :] = jnp.where(keep, turned[j], turned[j + 1])
        return carry

    lax.fori_loop(0, SEG, cut, 0)

    group = 4
    cols = group * SEGP
    dims = (((1,), (1,)), ((), ()))
    half = lax.broadcasted_iota(jnp.int32, (NFREQ, LANES), 1) < SEGP

    def transform(g, carry):
        at = pl.ds(pl.multiple_of(g * cols, cols), cols)
        rows = jnp.concatenate([frames[j, at, :] for j in range(width)], axis=1)
        top = rows.astype(jnp.bfloat16)
        rest = (rows - top.astype(jnp.float32)).astype(jnp.bfloat16)
        parts = []
        for p in range(2):
            hi = high_ref[p * NFREQ : (p + 1) * NFREQ, :]
            lo = low_ref[p * NFREQ : (p + 1) * NFREQ, :]
            value = lax.dot_general(hi, rest, dims, preferred_element_type=jnp.float32)
            value += lax.dot_general(lo, top, dims, preferred_element_type=jnp.float32)
            value += lax.dot_general(hi, top, dims, preferred_element_type=jnp.float32)
            parts.append(value)
        re, im = parts
        power = re * re + im * im
        band = jnp.mean(power.reshape(NFREQ // WBAND, WBAND, cols), axis=1, keepdims=True)
        scale = 1.0 / jnp.sqrt(band + 1e-06)
        scale = jnp.broadcast_to(scale, (NFREQ // WBAND, WBAND, cols)).reshape(NFREQ, cols)
        re = re * scale
        im = im * scale
        for h in range(group // 2):
            a = re[:, h * LANES : (h + 1) * LANES]
            b = im[:, h * LANES : (h + 1) * LANES]
            c = g * group + 2 * h
            even = pl.multiple_of(c * NFREQ, NFREQ)
            spread[pl.ds(even, NFREQ), :] = jnp.where(half, a, pltpu.roll(b, SEGP, 1))
            odd = pl.multiple_of((c + 1) * NFREQ, NFREQ)
            spread[pl.ds(odd, NFREQ), :] = jnp.where(half, pltpu.roll(a, SEGP, 1), b)
        return carry

    lax.fori_loop(0, sub // group, transform, 0)

    def regroup(f, carry):
        for u in range(8):
            k = f * 8 + u
            out_ref[k] = spread[pl.ds(k, sub, stride=NFREQ), :].astype(jnp.bfloat16)
        return carry

    lax.fori_loop(0, NFREQ // 8, regroup, 0)


def spectra(starts, received, chan_count, tm_count):
    sub = received.shape[1]
    high, low = windowed_table()
    vmem = pl.BlockSpec(memory_space=pltpu.VMEM)
    return pl.pallas_call(
        functools.partial(spectra_kernel, chan_count, tm_count),
        out_shape=jax.ShapeDtypeStruct((NFREQ, sub, LANES), jnp.bfloat16),
        in_specs=[pl.BlockSpec(memory_space=pltpu.SMEM), vmem, vmem, vmem],
        out_specs=vmem,
        scratch_shapes=[
            pltpu.VMEM((NFFT // LANES, sub * SEGP, LANES), jnp.float32),
            pltpu.VMEM((sub * NFREQ, LANES), jnp.float32),
        ],
        compiler_params=pltpu.CompilerParams(vmem_limit_bytes=VMEM_LIMIT),
    )(starts, received, jnp.asarray(high), jnp.asarray(low))


def compact_kernel(in_ref, pick_ref, out_ref):
    pieces, freqs, sub, _ = in_ref.shape
    block = pieces * sub
    dims = (((1,), (1,)), ((), ()))

    def one(g, carry):
        wide = jnp.concatenate(
            [
                jnp.concatenate([in_ref[p, g * QUAD + q] for p in range(pieces)], axis=0)
                for q in range(QUAD)
            ],
            axis=1,
        )
        value = lax.dot_general(pick_ref[...], wide, dims, preferred_element_type=jnp.float32)
        out_ref[g] = value.astype(jnp.bfloat16)
        return carry

    lax.fori_loop(0, freqs // QUAD, one, 0)


def compact(banded):
    pieces, freqs, sub, _ = banded.shape
    vmem = pl.BlockSpec(memory_space=pltpu.VMEM)
    return pl.pallas_call(
        compact_kernel,
        out_shape=jax.ShapeDtypeStruct((freqs // QUAD, QUAD * KROWS, pieces * sub), jnp.bfloat16),
        in_specs=[vmem, vmem],
        out_specs=vmem,
        compiler_params=pltpu.CompilerParams(vmem_limit_bytes=VMEM_LIMIT),
    )(banded, jnp.asarray(pick_table()))


def product_kernel(needed_ref, live_ref, left_ref, right_ref, out_ref):
    slot = pl.program_id(0)
    quads = left_ref.shape[1]
    block = left_ref.shape[3]
    norm = 1.0 / math.sqrt(SEG)
    dims = (((0,), (0,)), ((), ()))

    @pl.when(live_ref[slot] != 0)
    def _():
        def one(g, carry):
            left4 = left_ref[0, g]
            right4 = right_ref[0, g]
            for q in range(QUAD):
                left = left4[q * KROWS : (q + 1) * KROWS]
                right = right4[q * KROWS : (q + 1) * KROWS]
                turned = jnp.concatenate([-right[SEG:], right[:SEG]], axis=0)
                both = jnp.concatenate([right, turned], axis=1)
                value = lax.dot_general(left, both, dims, preferred_element_type=jnp.float32)
                value = (value * norm).astype(jnp.bfloat16)
                out_ref[0, g * QUAD + q, 0] = value[:, :block]
                out_ref[0, g * QUAD + q, 1] = value[:, block:]
            return carry

        lax.fori_loop(0, quads, one, 0)

    @pl.when(live_ref[slot] == 0)
    def _():
        out_ref[...] = jnp.zeros_like(out_ref)


def products(held, needed, live):
    _, groups, rows, block = held.shape
    step = 4
    freqs = groups * QUAD
    return pl.pallas_call(
        product_kernel,
        out_shape=jax.ShapeDtypeStruct((PMAX, freqs, 2, block, block), jnp.bfloat16),
        grid_spec=pltpu.PrefetchScalarGridSpec(
            num_scalar_prefetch=2,
            grid=(PMAX, groups // step),
            in_specs=[
                pl.BlockSpec((1, step, rows, block), lambda s, g, need, live: (need[2 * s], g, 0, 0)),
                pl.BlockSpec((1, step, rows, block), lambda s, g, need, live: (need[2 * s + 1], g, 0, 0)),
            ],
            out_specs=pl.BlockSpec(
                (1, step * QUAD, 2, block, block), lambda s, g, need, live: (s, g, 0, 0, 0)
            ),
        ),
        compiler_params=pltpu.CompilerParams(vmem_limit_bytes=VMEM_LIMIT),
    )(needed, live, held, held)


def body(records, pairs, owners, starts):
    tm_count = lax.axis_size("tm")
    chan_count = lax.axis_size("chan")
    chans, samp_dev = records.shape
    block = chans // chan_count
    sub = block // tm_count
    group_freq = NFREQ // tm_count
    moved = records.reshape(chan_count * tm_count, sub, samp_dev)
    received = lax.all_to_all(moved, ("chan", "tm"), split_axis=0, concat_axis=0, tiled=True)
    white = spectra(starts, received, chan_count, tm_count)
    white = white.reshape(tm_count, group_freq, sub, LANES)
    banded = lax.all_to_all(white, "tm", split_axis=0, concat_axis=0, tiled=True)
    local = compact(banded)
    held = lax.all_gather(local[None], "chan", axis=0, tiled=True)
    pair_id, live = slot_table(owners, chan_count)
    me_chan = lax.axis_index("chan")
    mine = lax.dynamic_slice_in_dim(pair_id, me_chan * PMAX, PMAX)
    my_live = lax.dynamic_slice_in_dim(live, me_chan * PMAX, PMAX).astype(jnp.int32)
    needed = pairs[mine].reshape(2 * PMAX)
    return products(held, needed, my_live)


def solution(mesh):
    return jax.shard_map(
        body,
        mesh=mesh,
        in_specs=(P(None, ("tm", "chan")), P(), P(), P()),
        out_specs=P("chan", "tm", None, None, None),
        check_vma=False,
    )
```

```python
import functools
import math
import jax
import jax.numpy as jnp
import ml_dtypes
import numpy as np
from jax import lax
from jax.experimental import pallas as pl
from jax.experimental.pallas import tpu as pltpu
from jax.sharding import PartitionSpec as P

NFFT = 1024
NFREQ = 384
WBAND = 64
SEG = 58
SEGP = 64
PMAX = 6
LANES = 128
KROWS = 2 * SEG
QUAD = 4
VMEM_LIMIT = 56 * 1024 * 1024
THIRDS = 3
STREAMS = 2
MAX_ROUNDS = 32
ROUND_CHOICES = (7, 8, 9)


def windowed_table():
    sample = np.arange(NFFT)
    freq = np.arange(NFREQ)
    angle = 2.0 * np.pi * ((freq[:, None] * sample[None, :]) % NFFT) / NFFT
    window = 0.5 - 0.5 * np.cos(2.0 * np.pi * sample / NFFT)
    table = np.concatenate([np.cos(angle), -np.sin(angle)], axis=0) * window[None, :]
    high = table.astype(np.float32).astype(ml_dtypes.bfloat16)
    low = (table - high.astype(np.float64)).astype(np.float32).astype(ml_dtypes.bfloat16)
    return high, low


def pick_table():
    pick = np.zeros((QUAD * KROWS, QUAD * LANES), np.float32)
    for q in range(QUAD):
        for part in range(2):
            for s in range(SEG):
                pick[q * KROWS + part * SEG + s, q * LANES + part * SEGP + s] = 1.0
    return pick.astype(ml_dtypes.bfloat16)


def slot_table(owners, owner_count):
    owner = owners[:, 0]
    npair = owner.shape[0]
    order = jnp.arange(npair, dtype=jnp.int32)
    same = owner[:, None] == owner[None, :]
    before = order[None, :] < order[:, None]
    rank = jnp.sum((same & before).astype(jnp.int32), axis=1)
    target = owner * PMAX + rank
    rows = jnp.arange(owner_count * PMAX, dtype=jnp.int32)
    match = target[None, :] == rows[:, None]
    live = jnp.any(match, axis=1)
    pair_id = jnp.sum(jnp.where(match, order[None, :], 0), axis=1)
    return (pair_id, live)


def spectra_kernel(chan_count, tm_count, starts_ref, rec_ref, high_ref, low_ref, out_ref, frames, spread):
    sub = rec_ref.shape[1]
    tiles = rec_ref.shape[2] // LANES
    total_tiles = rec_ref.shape[0] * tiles
    width = NFFT // LANES
    lane = lax.broadcasted_iota(jnp.int32, (sub, LANES), 1)
    for c in range(sub):
        frames[:, c * SEGP + SEG : (c + 1) * SEGP, :] = jnp.zeros(
            (width, SEGP - SEG, LANES), jnp.float32
        )

    def cut(s, carry):
        begin = starts_ref[s]
        base = jnp.minimum(begin // LANES, total_tiles - width - 1)
        over = begin - base * LANES
        shift = (LANES - over) % LANES
        turned = []
        for j in range(width + 1):
            tile = base + j
            piece = tile // tiles
            source = (piece % chan_count) * tm_count + piece // chan_count
            at = pl.multiple_of((tile % tiles) * LANES, LANES)
            turned.append(pltpu.roll(rec_ref[source, :, pl.ds(at, LANES)], shift, 1))
        keep = lane < LANES - over
        for j in range(width):
            frames[j, pl.ds(s, sub, stride=SEGP), :] = jnp.where(keep, turned[j], turned[j + 1])
        return carry

    lax.fori_loop(0, SEG, cut, 0)

    group = 4
    cols = group * SEGP
    dims = (((1,), (1,)), ((), ()))
    half = lax.broadcasted_iota(jnp.int32, (NFREQ, LANES), 1) < SEGP

    def transform(g, carry):
        at = pl.ds(pl.multiple_of(g * cols, cols), cols)
        rows = jnp.concatenate([frames[j, at, :] for j in range(width)], axis=1)
        top = rows.astype(jnp.bfloat16)
        rest = (rows - top.astype(jnp.float32)).astype(jnp.bfloat16)
        parts = []
        for p in range(2):
            hi = high_ref[p * NFREQ : (p + 1) * NFREQ, :]
            lo = low_ref[p * NFREQ : (p + 1) * NFREQ, :]
            value = lax.dot_general(hi, rest, dims, preferred_element_type=jnp.float32)
            value += lax.dot_general(lo, top, dims, preferred_element_type=jnp.float32)
            value += lax.dot_general(hi, top, dims, preferred_element_type=jnp.float32)
            parts.append(value)
        re, im = parts
        power = re * re + im * im
        band = jnp.mean(power.reshape(NFREQ // WBAND, WBAND, cols), axis=1, keepdims=True)
        scale = 1.0 / jnp.sqrt(band + 1e-06)
        scale = jnp.broadcast_to(scale, (NFREQ // WBAND, WBAND, cols)).reshape(NFREQ, cols)
        re = re * scale
        im = im * scale
        for h in range(group // 2):
            a = re[:, h * LANES : (h + 1) * LANES]
            b = im[:, h * LANES : (h + 1) * LANES]
            c = g * group + 2 * h
            even = pl.multiple_of(c * NFREQ, NFREQ)
            spread[pl.ds(even, NFREQ), :] = jnp.where(half, a, pltpu.roll(b, SEGP, 1))
            odd = pl.multiple_of((c + 1) * NFREQ, NFREQ)
            spread[pl.ds(odd, NFREQ), :] = jnp.where(half, pltpu.roll(a, SEGP, 1), b)
        return carry

    lax.fori_loop(0, sub // group, transform, 0)

    def regroup(f, carry):
        for u in range(8):
            k = f * 8 + u
            out_ref[k] = spread[pl.ds(k, sub, stride=NFREQ), :].astype(jnp.bfloat16)
        return carry

    lax.fori_loop(0, NFREQ // 8, regroup, 0)


def spectra(starts, received, chan_count, tm_count):
    sub = received.shape[1]
    high, low = windowed_table()
    vmem = pl.BlockSpec(memory_space=pltpu.VMEM)
    return pl.pallas_call(
        functools.partial(spectra_kernel, chan_count, tm_count),
        out_shape=jax.ShapeDtypeStruct((NFREQ, sub, LANES), jnp.bfloat16),
        in_specs=[pl.BlockSpec(memory_space=pltpu.SMEM), vmem, vmem, vmem],
        out_specs=vmem,
        scratch_shapes=[
            pltpu.VMEM((NFFT // LANES, sub * SEGP, LANES), jnp.float32),
            pltpu.VMEM((sub * NFREQ, LANES), jnp.float32),
        ],
        compiler_params=pltpu.CompilerParams(vmem_limit_bytes=VMEM_LIMIT),
    )(starts, received, jnp.asarray(high), jnp.asarray(low))


def compact_kernel(in_ref, pick_ref, out_ref):
    pieces, freqs, sub, _ = in_ref.shape
    block = pieces * sub
    dims = (((1,), (1,)), ((), ()))

    def one(g, carry):
        wide = jnp.concatenate(
            [
                jnp.concatenate([in_ref[p, g * QUAD + q] for p in range(pieces)], axis=0)
                for q in range(QUAD)
            ],
            axis=1,
        )
        value = lax.dot_general(pick_ref[...], wide, dims, preferred_element_type=jnp.float32)
        out_ref[g] = value.astype(jnp.bfloat16)
        return carry

    lax.fori_loop(0, freqs // QUAD, one, 0)


def compact(banded):
    pieces, freqs, sub, _ = banded.shape
    vmem = pl.BlockSpec(memory_space=pltpu.VMEM)
    return pl.pallas_call(
        compact_kernel,
        out_shape=jax.ShapeDtypeStruct((freqs // QUAD, QUAD * KROWS, pieces * sub), jnp.bfloat16),
        in_specs=[vmem, vmem],
        out_specs=vmem,
        compiler_params=pltpu.CompilerParams(vmem_limit_bytes=VMEM_LIMIT),
    )(banded, jnp.asarray(pick_table()))


def torus_tables(count):
    side = math.isqrt(count)
    index = np.arange(count)
    x, y = index // side, index % side
    sources = [
        (x + 1) % side * side + y,
        (x - 1) % side * side + y,
        x * side + (y + 1) % side,
        x * side + (y - 1) % side,
    ]
    near = np.concatenate([np.eye(count)[source] for source in sources], axis=0)
    dx = np.abs(x[:, None] - x[None, :])
    dy = np.abs(y[:, None] - y[None, :])
    dist = np.minimum(dx, side - dx) + np.minimum(dy, side - dy)
    reach = np.concatenate([dist <= d for d in range(4)], axis=0)
    shell = np.concatenate([(dist == d) * 2.0 ** (3 - d) for d in range(4)], axis=1)
    return [t.astype(ml_dtypes.bfloat16) for t in (near, reach, shell)]


def plan_kernel(pairs_ref, owners_ref, near_ref, reach_ref, shell_ref, table_ref, slots_ref, rounds_ref):
    count = near_ref.shape[1]
    shape = (count, LANES)
    node = lax.broadcasted_iota(jnp.int32, shape, 0)
    lane = lax.broadcasted_iota(jnp.int32, shape, 1)
    inside = lane < THIRDS * count
    block = lane % count
    third = lane // count
    commodities = THIRDS * count
    tie = commodities - 1 - (lane + 3 * node) % commodities
    tie = jnp.where(inside, tie, 0).astype(jnp.float32)

    def mark(p, need):
        hit = (block == pairs_ref[p, 0]) | (block == pairs_ref[p, 1])
        return jnp.where(hit & (node == owners_ref[p, 0]) & inside, 1.0, need)

    need = lax.fori_loop(0, pairs_ref.shape[0], mark, jnp.zeros(shape, jnp.float32))
    has = jnp.where((block == node) & inside, 1.0, 0.0)
    slot_of = jnp.where(has > 0, third, 0).astype(jnp.float32)
    table = jnp.zeros(shape, jnp.float32)

    def dot(m, v):
        return jnp.dot(m, v.astype(jnp.bfloat16), preferred_element_type=jnp.float32)

    def unfinished(state):
        r, left, _, _, _ = state
        return (left > 0) & (r < MAX_ROUNDS)

    def one(state):
        r, _, has, slot_of, table = state
        rem = need * (1.0 - has)
        short = rem * jnp.sum(rem, axis=1, keepdims=True)
        reached = dot(reach_ref[...], has)
        waves = jnp.concatenate(
            [jnp.where(reached[d * count : (d + 1) * count] > 0, 0.0, short) for d in range(4)], axis=0
        )
        gain = dot(shell_ref[...], waves)
        both = dot(near_ref[...], jnp.concatenate([has, slot_of], axis=1))
        near_has = [both[k * count : (k + 1) * count, :LANES] for k in range(4)]
        near_slot = [both[k * count : (k + 1) * count, LANES:] for k in range(4)]
        sources = near_has[0] + near_has[1] + near_has[2] + near_has[3]
        worth = jnp.where((gain > 0) & (has == 0), gain * (5.0 - sources) * 64.0 + tie, 0.0)
        for k in range(4):
            key = worth * near_has[k]
            best = jnp.max(key, axis=1, keepdims=True)
            chosen = (key == best) & (key > 0)
            worth = jnp.where(chosen, 0.0, worth)
            has = jnp.where(chosen, 1.0, has)
            source = jnp.sum(jnp.where(chosen, near_slot[k], 0.0), axis=1, keepdims=True)
            table = jnp.where(lane == 4 * r + k, source, table)
            slot_of = jnp.where(chosen, (THIRDS + 4 * r + k).astype(jnp.float32), slot_of)
        left = jnp.sum(need * (1.0 - has))
        return r + 1, left, has, slot_of, table

    left = jnp.sum(need * (1.0 - has))
    rounds, left, has, slot_of, table = lax.while_loop(
        unfinished, one, (jnp.int32(0), left, has, slot_of, table)
    )
    table_ref[...] = table.astype(jnp.int32)
    slots_ref[...] = slot_of.astype(jnp.int32)
    rounds_ref[...] = jnp.full(rounds_ref.shape, jnp.where(left > 0, MAX_ROUNDS, rounds), jnp.int32)


def plan(pairs, owners, count):
    near, reach, shell = torus_tables(count)
    vmem = pl.BlockSpec(memory_space=pltpu.VMEM)
    smem = pl.BlockSpec(memory_space=pltpu.SMEM)
    grid = jax.ShapeDtypeStruct((count, LANES), jnp.int32)
    return pl.pallas_call(
        plan_kernel,
        out_shape=(grid, grid, jax.ShapeDtypeStruct((8, LANES), jnp.int32)),
        in_specs=[smem, smem, vmem, vmem, vmem],
        out_specs=(vmem, vmem, vmem),
    )(pairs, owners, jnp.asarray(near), jnp.asarray(reach), jnp.asarray(shell))


def exchange_kernel(count, rounds, table_ref, own_ref, out_ref, held, land, stage, send_sem, recv_sem, out_sem):
    side = math.isqrt(count)
    me = lax.axis_index("chan")
    x, y = me // side, me % side
    targets = [
        (x + side - 1) % side * side + y,
        (x + 1) % side * side + y,
        x * side + (y + side - 1) % side,
        x * side + (y + 1) % side,
    ]
    rows = own_ref.shape[2]
    step = 32

    barrier = pltpu.get_barrier_semaphore()
    for k in range(4):
        pl.semaphore_signal(
            barrier, inc=1, device_id={"chan": targets[k]}, device_id_type=pl.DeviceIdType.MESH
        )
    pl.semaphore_wait(barrier, 4)

    def each_chunk(work):
        def run(i, carry):
            work(pl.ds(pl.multiple_of(i * step, step), step))
            return carry

        lax.fori_loop(0, rows // step, run, 0)

    def remote(parity, h, k):
        return pltpu.make_async_remote_copy(
            src_ref=stage.at[parity, h, k],
            dst_ref=land.at[parity, h, k],
            send_sem=send_sem.at[parity, h, k],
            recv_sem=recv_sem.at[parity, h, k],
            device_id={"chan": targets[k]},
            device_id_type=pl.DeviceIdType.MESH,
        )

    def keep_own(h):
        return pltpu.make_async_copy(
            own_ref.at[:, h], out_ref.at[pl.ds(0, THIRDS), h], out_sem.at[rounds, h]
        )

    def keep(r, h):
        at = pl.ds(THIRDS + 4 * r, 4)
        return pltpu.make_async_copy(held.at[at, h], out_ref.at[at, h], out_sem.at[r, h])

    def absorb(r, h):
        parity = r % 2
        for k in range(4):
            remote(parity, h, k).wait_recv()

        def work(at):
            for k in range(4):
                held[THIRDS + 4 * r + k, h, at, :] = land[parity, h, k, at, :]

        each_chunk(work)
        keep(r, h).start()

    def send(r, h):
        parity = r % 2
        source = [table_ref[targets[k], 4 * r + k] for k in range(4)]

        def work(at):
            for k in range(4):
                stage[parity, h, k, at, :] = held[source[k], h, at, :]

        each_chunk(work)
        for k in range(4):
            remote(parity, h, k).start()

    for h in range(STREAMS):

        def work(at):
            for s in range(THIRDS):
                held[s, h, at, :] = own_ref[s, h, at, :]

        each_chunk(work)
        send(0, h)
        keep_own(h).start()
    for h in range(STREAMS):
        absorb(0, h)
        send(1, h)

    def general(r, carry):
        for h in range(STREAMS):
            absorb(r - 1, h)
            for k in range(4):
                remote(r % 2, h, k).wait_send()
            send(r, h)
        return carry

    lax.fori_loop(2, rounds, general, 0)
    for h in range(STREAMS):
        absorb(rounds - 1, h)
        for parity in range(2):
            for k in range(4):
                remote(parity, h, k).wait_send()
    for h in range(STREAMS):
        keep_own(h).wait()
        for r in range(rounds):
            keep(r, h).wait()


def exchange(table, own, count, rounds, ident):
    _, streams, rows, block = own.shape
    return pl.pallas_call(
        functools.partial(exchange_kernel, count, rounds),
        out_shape=jax.ShapeDtypeStruct((THIRDS * count, streams, rows, block), own.dtype),
        in_specs=[pl.BlockSpec(memory_space=pltpu.SMEM), pl.BlockSpec(memory_space=pltpu.VMEM)],
        out_specs=pl.BlockSpec(memory_space=pl.ANY),
        scratch_shapes=[
            pltpu.VMEM((THIRDS + 4 * rounds, streams, rows, block), own.dtype),
            pltpu.VMEM((2, streams, 4, rows, block), own.dtype),
            pltpu.VMEM((2, streams, 4, rows, block), own.dtype),
            pltpu.SemaphoreType.DMA((2, streams, 4)),
            pltpu.SemaphoreType.DMA((2, streams, 4)),
            pltpu.SemaphoreType.DMA((rounds + 1, streams)),
        ],
        compiler_params=pltpu.CompilerParams(
            vmem_limit_bytes=VMEM_LIMIT, collective_id=ident, has_side_effects=True
        ),
    )(table, own)


def gather_needed(table, slots, rounds, own, me, count):
    mine = lax.dynamic_index_in_dim(slots, me, 0, keepdims=False)
    every = np.arange(LANES)
    every = np.where(every < THIRDS * count, every % count * THIRDS + every // count, 0)
    every = jnp.asarray(every, jnp.int32)

    def by_rounds(choice, ident):
        return lambda: (exchange(table, own, count, choice, ident), mine)

    def whole():
        return lax.all_gather(own, "chan", axis=0, tiled=True), every

    branches = [by_rounds(choice, i) for i, choice in enumerate(ROUND_CHOICES)] + [whole]
    which = sum((rounds > choice).astype(jnp.int32) for choice in ROUND_CHOICES)
    return lax.switch(which, branches)


def product_kernel(needed_ref, live_ref, left_ref, right_ref, out_ref):
    slot = pl.program_id(0)
    streams, rows, block = left_ref.shape[1:]
    norm = 1.0 / math.sqrt(SEG)
    dims = (((0,), (0,)), ((), ()))
    per = rows // (QUAD * KROWS)

    @pl.when(live_ref[slot] != 0)
    def _():
        def one(g, carry):
            at = pl.ds(pl.multiple_of(g % per * (QUAD * KROWS), 16), QUAD * KROWS)
            left4 = left_ref[0, g // per, at]
            right4 = right_ref[0, g // per, at]
            for q in range(QUAD):
                left = left4[q * KROWS : (q + 1) * KROWS]
                right = right4[q * KROWS : (q + 1) * KROWS]
                turned = jnp.concatenate([-right[SEG:], right[:SEG]], axis=0)
                both = jnp.concatenate([right, turned], axis=1)
                value = lax.dot_general(left, both, dims, preferred_element_type=jnp.float32)
                value = (value * norm).astype(jnp.bfloat16)
                out_ref[0, g * QUAD + q, 0] = value[:, :block]
                out_ref[0, g * QUAD + q, 1] = value[:, block:]
            return carry

        lax.fori_loop(0, streams * per, one, 0)

    @pl.when(live_ref[slot] == 0)
    def _():
        out_ref[...] = jnp.zeros_like(out_ref)


def products(held, needed, live):
    _, streams, rows, block = held.shape
    part = streams * rows // KROWS
    spec = (1, streams, rows, block)
    return pl.pallas_call(
        product_kernel,
        out_shape=jax.ShapeDtypeStruct((PMAX, THIRDS * part, 2, block, block), jnp.bfloat16),
        grid_spec=pltpu.PrefetchScalarGridSpec(
            num_scalar_prefetch=2,
            grid=(PMAX, THIRDS),
            in_specs=[
                pl.BlockSpec(spec, lambda s, g, need, live: (need[2 * s, g], 0, 0, 0)),
                pl.BlockSpec(spec, lambda s, g, need, live: (need[2 * s + 1, g], 0, 0, 0)),
            ],
            out_specs=pl.BlockSpec((1, part, 2, block, block), lambda s, g, need, live: (s, g, 0, 0, 0)),
        ),
        compiler_params=pltpu.CompilerParams(vmem_limit_bytes=VMEM_LIMIT),
    )(needed, live, held, held)


def body(records, pairs, owners, starts):
    tm_count = lax.axis_size("tm")
    chan_count = lax.axis_size("chan")
    chans, samp_dev = records.shape
    block = chans // chan_count
    sub = block // tm_count
    group_freq = NFREQ // tm_count
    table, slots, rounds = plan(pairs, owners, chan_count)
    moved = records.reshape(chan_count * tm_count, sub, samp_dev)
    received = lax.all_to_all(moved, ("chan", "tm"), split_axis=0, concat_axis=0, tiled=True)
    white = spectra(starts, received, chan_count, tm_count)
    white = white.reshape(tm_count, group_freq, sub, LANES)
    banded = lax.all_to_all(white, "tm", split_axis=0, concat_axis=0, tiled=True)
    own = compact(banded).reshape(THIRDS, STREAMS, -1, block)
    me_chan = lax.axis_index("chan")
    held, slot_of = gather_needed(table, slots, rounds[0, 0], own, me_chan, chan_count)
    pair_id, live = slot_table(owners, chan_count)
    mine = lax.dynamic_slice_in_dim(pair_id, me_chan * PMAX, PMAX)
    my_live = lax.dynamic_slice_in_dim(live, me_chan * PMAX, PMAX).astype(jnp.int32)
    blocks = pairs[mine].reshape(2 * PMAX)
    needed = slot_of[blocks[:, None] + chan_count * jnp.arange(THIRDS, dtype=jnp.int32)[None, :]]
    return products(held, needed, my_live)


def solution(mesh):
    return jax.shard_map(
        body,
        mesh=mesh,
        in_specs=(P(None, ("tm", "chan")), P(), P(), P()),
        out_specs=P("chan", "tm", None, None, None),
        check_vma=False,
    )
```

```python
import functools
import math
import jax
import jax.numpy as jnp
import ml_dtypes
import numpy as np
from jax import lax
from jax.experimental import pallas as pl
from jax.experimental.pallas import tpu as pltpu
from jax.sharding import PartitionSpec as P

NFFT = 1024
NFREQ = 384
WBAND = 64
SEG = 58
SEGP = 64
PMAX = 6
LANES = 128
KROWS = 2 * SEG
QUAD = 4
VMEM_LIMIT = 56 * 1024 * 1024
EXCHANGE_LIMIT = 28 * 1024 * 1024
PRODUCT_LIMIT = 12 * 1024 * 1024
THIRDS = 3
STREAMS = 2
MAX_ROUNDS = 32
ROUND_CHOICES = (7, 8)
SCALE = 8192.0


def windowed_table():
    sample = np.arange(NFFT)
    freq = np.arange(NFREQ)
    angle = 2.0 * np.pi * ((freq[:, None] * sample[None, :]) % NFFT) / NFFT
    window = 0.5 - 0.5 * np.cos(2.0 * np.pi * sample / NFFT)
    table = np.concatenate([np.cos(angle), -np.sin(angle)], axis=0) * window[None, :] / SCALE
    high = table.astype(np.float32).astype(ml_dtypes.bfloat16)
    low = (table - high.astype(np.float64)).astype(np.float32).astype(ml_dtypes.bfloat16)
    return high, low


def pick_table():
    pick = np.zeros((QUAD * KROWS, QUAD * LANES), np.float32)
    for q in range(QUAD):
        for part in range(2):
            for s in range(SEG):
                pick[q * KROWS + part * SEG + s, q * LANES + part * SEGP + s] = 1.0
    return pick.astype(ml_dtypes.bfloat16)


def slot_table(owners, owner_count):
    owner = owners[:, 0]
    npair = owner.shape[0]
    order = jnp.arange(npair, dtype=jnp.int32)
    same = owner[:, None] == owner[None, :]
    before = order[None, :] < order[:, None]
    rank = jnp.sum((same & before).astype(jnp.int32), axis=1)
    target = owner * PMAX + rank
    rows = jnp.arange(owner_count * PMAX, dtype=jnp.int32)
    match = target[None, :] == rows[:, None]
    live = jnp.any(match, axis=1)
    pair_id = jnp.sum(jnp.where(match, order[None, :], 0), axis=1)
    return (pair_id, live)


def bits(size):
    assert size & (size - 1) == 0
    return size.bit_length() - 1


def spectra_kernel(
    chan_count, tm_count, starts_ref, rec_ref, high_hbm, low_hbm, out_ref, high_ref, low_ref, frames, spread, sems
):
    fetch = [
        pltpu.make_async_copy(high_hbm, high_ref, sems.at[0]),
        pltpu.make_async_copy(low_hbm, low_ref, sems.at[1]),
    ]
    for copy in fetch:
        copy.start()
    sub = rec_ref.shape[1]
    tiles = rec_ref.shape[2] // LANES
    total_tiles = rec_ref.shape[0] * tiles
    width = NFFT // LANES
    lane = lax.broadcasted_iota(jnp.int32, (sub, LANES), 1)
    for c in range(sub):
        frames[:, c * SEGP + SEG : (c + 1) * SEGP, :] = jnp.zeros(
            (width, SEGP - SEG, LANES), jnp.float32
        )

    def cut(s, carry):
        begin = starts_ref[s]
        base = jnp.minimum(begin >> bits(LANES), total_tiles - width - 1)
        over = begin - base * LANES
        shift = (LANES - over) & (LANES - 1)
        turned = []
        for j in range(width + 1):
            tile = base + j
            piece = tile >> bits(tiles)
            source = (piece & (chan_count - 1)) * tm_count + (piece >> bits(chan_count))
            at = pl.multiple_of((tile & (tiles - 1)) * LANES, LANES)
            turned.append(pltpu.roll(rec_ref[source, :, pl.ds(at, LANES)], shift, 1))
        keep = lane < LANES - over
        for j in range(width):
            frames[j, pl.ds(s, sub, stride=SEGP), :] = jnp.where(keep, turned[j], turned[j + 1])
        return carry

    lax.fori_loop(0, SEG, cut, 0, unroll=2)
    for copy in fetch:
        copy.wait()

    group = 4
    cols = group * SEGP
    dims = (((1,), (1,)), ((), ()))
    half = lax.broadcasted_iota(jnp.int32, (NFREQ, LANES), 1) < SEGP

    def transform(g, carry):
        at = pl.ds(pl.multiple_of(g * cols, cols), cols)
        rows = jnp.concatenate([frames[j, at, :] for j in range(width)], axis=1)
        top = rows.astype(jnp.bfloat16)
        rest = (rows - top.astype(jnp.float32)).astype(jnp.bfloat16)
        parts = []
        for p in range(2):
            hi = high_ref[p * NFREQ : (p + 1) * NFREQ, :]
            lo = low_ref[p * NFREQ : (p + 1) * NFREQ, :]
            value = lax.dot_general(hi, rest, dims, preferred_element_type=jnp.float32)
            value += lax.dot_general(lo, top, dims, preferred_element_type=jnp.float32)
            value += lax.dot_general(hi, top, dims, preferred_element_type=jnp.float32)
            parts.append(value)
        re, im = parts
        power = re * re + im * im
        band = jnp.mean(power.reshape(NFREQ // WBAND, WBAND, cols), axis=1, keepdims=True)
        scale = 1.0 / jnp.sqrt(band + 1e-06)
        scale = jnp.broadcast_to(scale, (NFREQ // WBAND, WBAND, cols)).reshape(NFREQ, cols)
        re = re * scale
        im = im * scale
        for h in range(group // 2):
            a = re[:, h * LANES : (h + 1) * LANES]
            b = im[:, h * LANES : (h + 1) * LANES]
            c = g * group + 2 * h
            even = pl.multiple_of(c * NFREQ, NFREQ)
            spread[pl.ds(even, NFREQ), :] = jnp.where(half, a, pltpu.roll(b, SEGP, 1))
            odd = pl.multiple_of((c + 1) * NFREQ, NFREQ)
            spread[pl.ds(odd, NFREQ), :] = jnp.where(half, pltpu.roll(a, SEGP, 1), b)
        return carry

    lax.fori_loop(0, sub // group, transform, 0)

    def regroup(f, carry):
        for u in range(8):
            k = f * 8 + u
            out_ref[k] = spread[pl.ds(k, sub, stride=NFREQ), :].astype(jnp.bfloat16)
        return carry

    lax.fori_loop(0, NFREQ // 8, regroup, 0)


def spectra(starts, received, chan_count, tm_count):
    sub = received.shape[1]
    high, low = windowed_table()
    vmem = pl.BlockSpec(memory_space=pltpu.VMEM)
    return pl.pallas_call(
        functools.partial(spectra_kernel, chan_count, tm_count),
        out_shape=jax.ShapeDtypeStruct((NFREQ, sub, LANES), jnp.bfloat16),
        in_specs=[
            pl.BlockSpec(memory_space=pltpu.SMEM),
            vmem,
            pl.BlockSpec(memory_space=pl.ANY),
            pl.BlockSpec(memory_space=pl.ANY),
        ],
        out_specs=vmem,
        scratch_shapes=[
            pltpu.VMEM(high.shape, high.dtype),
            pltpu.VMEM(low.shape, low.dtype),
            pltpu.VMEM((NFFT // LANES, sub * SEGP, LANES), jnp.float32),
            pltpu.VMEM((sub * NFREQ, LANES), jnp.float32),
            pltpu.SemaphoreType.DMA((2,)),
        ],
        compiler_params=pltpu.CompilerParams(vmem_limit_bytes=VMEM_LIMIT),
    )(starts, received, jnp.asarray(high), jnp.asarray(low))


def compact_kernel(in_ref, pick_ref, out_ref):
    pieces, freqs, sub, _ = in_ref.shape
    block = pieces * sub
    dims = (((1,), (1,)), ((), ()))

    def one(g, carry):
        wide = jnp.concatenate(
            [
                jnp.concatenate([in_ref[p, g * QUAD + q] for p in range(pieces)], axis=0)
                for q in range(QUAD)
            ],
            axis=1,
        )
        value = lax.dot_general(pick_ref[...], wide, dims, preferred_element_type=jnp.float32)
        out_ref[g] = value.astype(jnp.bfloat16)
        return carry

    lax.fori_loop(0, freqs // QUAD, one, 0)


def compact(banded):
    pieces, freqs, sub, _ = banded.shape
    vmem = pl.BlockSpec(memory_space=pltpu.VMEM)
    return pl.pallas_call(
        compact_kernel,
        out_shape=jax.ShapeDtypeStruct((freqs // QUAD, QUAD * KROWS, pieces * sub), jnp.bfloat16),
        in_specs=[vmem, vmem],
        out_specs=vmem,
        compiler_params=pltpu.CompilerParams(vmem_limit_bytes=VMEM_LIMIT),
    )(banded, jnp.asarray(pick_table()))


def torus_tables(count):
    side = math.isqrt(count)
    index = np.arange(count)
    x, y = index // side, index % side
    sources = [
        (x + 1) % side * side + y,
        (x - 1) % side * side + y,
        x * side + (y + 1) % side,
        x * side + (y - 1) % side,
    ]
    near = np.concatenate([np.eye(count)[source] for source in sources], axis=0)
    dx = np.abs(x[:, None] - x[None, :])
    dy = np.abs(y[:, None] - y[None, :])
    dist = np.minimum(dx, side - dx) + np.minimum(dy, side - dy)
    reach = np.concatenate([dist <= d for d in range(4)], axis=0)
    shell = np.concatenate([(dist == d) * 2.0 ** (3 - d) for d in range(4)], axis=1)
    return [t.astype(ml_dtypes.bfloat16) for t in (near, reach, shell)]


def plan_kernel(pairs_ref, owners_ref, near_ref, reach_ref, shell_ref, table_ref, slots_ref, rounds_ref):
    count = near_ref.shape[1]
    shape = (count, LANES)
    node = lax.broadcasted_iota(jnp.int32, shape, 0)
    lane = lax.broadcasted_iota(jnp.int32, shape, 1)
    inside = lane < THIRDS * count
    block = lane % count
    third = lane // count
    commodities = THIRDS * count
    tie = commodities - 1 - (lane + 3 * node) % commodities
    tie = jnp.where(inside, tie, 0).astype(jnp.float32)

    def mark(p, need):
        hit = (block == pairs_ref[p, 0]) | (block == pairs_ref[p, 1])
        return jnp.where(hit & (node == owners_ref[p, 0]) & inside, 1.0, need)

    need = lax.fori_loop(0, pairs_ref.shape[0], mark, jnp.zeros(shape, jnp.float32))
    has = jnp.where((block == node) & inside, 1.0, 0.0)
    slot_of = jnp.where(has > 0, third, 0).astype(jnp.float32)
    table = jnp.zeros(shape, jnp.float32)

    def dot(m, v):
        return jnp.dot(m, v.astype(jnp.bfloat16), preferred_element_type=jnp.float32)

    def unfinished(state):
        r, left, _, _, _ = state
        return (left > 0) & (r < MAX_ROUNDS)

    def one(state):
        r, _, has, slot_of, table = state
        rem = need * (1.0 - has)
        short = rem * jnp.sum(rem, axis=1, keepdims=True)
        reached = dot(reach_ref[...], has)
        waves = jnp.concatenate(
            [jnp.where(reached[d * count : (d + 1) * count] > 0, 0.0, short) for d in range(4)], axis=0
        )
        gain = dot(shell_ref[...], waves)
        both = dot(near_ref[...], jnp.concatenate([has, slot_of], axis=1))
        near_has = [both[k * count : (k + 1) * count, :LANES] for k in range(4)]
        near_slot = [both[k * count : (k + 1) * count, LANES:] for k in range(4)]
        sources = near_has[0] + near_has[1] + near_has[2] + near_has[3]
        worth = jnp.where((gain > 0) & (has == 0), gain * (5.0 - sources) * 64.0 + tie, 0.0)
        for k in range(4):
            key = worth * near_has[k]
            best = jnp.max(key, axis=1, keepdims=True)
            chosen = (key == best) & (key > 0)
            worth = jnp.where(chosen, 0.0, worth)
            has = jnp.where(chosen, 1.0, has)
            source = jnp.sum(jnp.where(chosen, near_slot[k], 0.0), axis=1, keepdims=True)
            table = jnp.where(lane == 4 * r + k, source, table)
            slot_of = jnp.where(chosen, (THIRDS + 4 * r + k).astype(jnp.float32), slot_of)
        left = jnp.sum(need * (1.0 - has))
        return r + 1, left, has, slot_of, table

    left = jnp.sum(need * (1.0 - has))
    rounds, left, has, slot_of, table = lax.while_loop(
        unfinished, one, (jnp.int32(0), left, has, slot_of, table)
    )
    table_ref[...] = table.astype(jnp.int32)
    slots_ref[...] = slot_of.astype(jnp.int32)
    rounds_ref[...] = jnp.full(rounds_ref.shape, jnp.where(left > 0, MAX_ROUNDS, rounds), jnp.int32)


def plan(pairs, owners, count):
    near, reach, shell = torus_tables(count)
    vmem = pl.BlockSpec(memory_space=pltpu.VMEM)
    smem = pl.BlockSpec(memory_space=pltpu.SMEM)
    grid = jax.ShapeDtypeStruct((count, LANES), jnp.int32)
    return pl.pallas_call(
        plan_kernel,
        out_shape=(grid, grid, jax.ShapeDtypeStruct((8, LANES), jnp.int32)),
        in_specs=[smem, smem, vmem, vmem, vmem],
        out_specs=(vmem, vmem, vmem),
    )(pairs, owners, jnp.asarray(near), jnp.asarray(reach), jnp.asarray(shell))


def exchange_kernel(
    count,
    bands,
    rounds,
    table_ref,
    white_ref,
    pick_ref,
    out_ref,
    held,
    spread,
    land,
    stage,
    send_sem,
    recv_sem,
    out_sem,
    band_send,
    band_recv,
    band_own,
):
    side = math.isqrt(count)
    me = lax.axis_index("chan")
    x, y = me // side, me % side
    targets = [
        (x + side - 1) % side * side + y,
        (x + 1) % side * side + y,
        x * side + (y + side - 1) % side,
        x * side + (y + 1) % side,
    ]
    rows = held.shape[2]
    sub = white_ref.shape[4]
    step = 32
    band = lax.axis_index("tm")

    barrier = pltpu.get_barrier_semaphore()
    for k in range(4):
        pl.semaphore_signal(
            barrier, inc=1, device_id={"chan": targets[k]}, device_id_type=pl.DeviceIdType.MESH
        )
    for i in range(1, bands):
        pl.semaphore_signal(
            barrier, inc=1, device_id={"tm": (band + i) % bands}, device_id_type=pl.DeviceIdType.MESH
        )
    pl.semaphore_wait(barrier, 4 + bands - 1)

    def place(source):
        return pl.ds(pl.multiple_of(source * sub, sub), sub)

    def to_band(h, i):
        target = (band + i) % bands
        return pltpu.make_async_remote_copy(
            src_ref=white_ref.at[target, :, h],
            dst_ref=spread.at[h, :, :, place(band)],
            send_sem=band_send.at[h, i],
            recv_sem=band_recv.at[h, i],
            device_id={"tm": target},
            device_id_type=pl.DeviceIdType.MESH,
        )

    def from_band(h, i):
        source = (band + bands - i) % bands
        return pltpu.make_async_remote_copy(
            src_ref=white_ref.at[source, :, h],
            dst_ref=spread.at[h, :, :, place(source)],
            send_sem=band_send.at[h, i],
            recv_sem=band_recv.at[h, i],
            device_id={"tm": source},
            device_id_type=pl.DeviceIdType.MESH,
        )

    def stay(h):
        return pltpu.make_async_copy(
            white_ref.at[band, :, h], spread.at[h, :, :, place(band)], band_own.at[h]
        )

    for h in range(STREAMS):
        for i in range(1, bands):
            to_band(h, i).start()
        stay(h).start()

    def each_chunk(work):
        def run(i, carry):
            work(pl.ds(pl.multiple_of(i * step, step), step))
            return carry

        lax.fori_loop(0, rows // step, run, 0)

    def remote(parity, h, k):
        return pltpu.make_async_remote_copy(
            src_ref=stage.at[parity, h, k],
            dst_ref=land.at[parity, h, k],
            send_sem=send_sem.at[parity, h, k],
            recv_sem=recv_sem.at[parity, h, k],
            device_id={"chan": targets[k]},
            device_id_type=pl.DeviceIdType.MESH,
        )

    def keep_own(h):
        return pltpu.make_async_copy(
            held.at[pl.ds(0, THIRDS), h], out_ref.at[pl.ds(0, THIRDS), h], out_sem.at[rounds, h]
        )

    def keep(r, h):
        at = pl.ds(THIRDS + 4 * r, 4)
        return pltpu.make_async_copy(held.at[at, h], out_ref.at[at, h], out_sem.at[r, h])

    def absorb(r, h):
        parity = r % 2
        for k in range(4):
            remote(parity, h, k).wait_recv()

        def work(at):
            for k in range(4):
                held[THIRDS + 4 * r + k, h, at, :] = land[parity, h, k, at, :]

        each_chunk(work)
        keep(r, h).start()

    def send(r, h):
        parity = r % 2
        source = [table_ref[targets[k], 4 * r + k] for k in range(4)]

        def work(at):
            for k in range(4):
                stage[parity, h, k, at, :] = held[source[k], h, at, :]

        each_chunk(work)
        for k in range(4):
            remote(parity, h, k).start()

    dims = (((1,), (1,)), ((), ()))
    quads = spread.shape[2] // QUAD

    for h in range(STREAMS):
        stay(h).wait()
        for i in range(1, bands):
            from_band(h, i).wait_recv()

        def turn(g, carry):
            s, part = g // quads, g % quads
            wide = jnp.concatenate([spread[h, s, part * QUAD + q] for q in range(QUAD)], axis=1)
            value = lax.dot_general(pick_ref[...], wide, dims, preferred_element_type=jnp.float32)
            at = pl.ds(pl.multiple_of(part * (QUAD * KROWS), QUAD * KROWS), QUAD * KROWS)
            held[s, h, at, :] = value.astype(jnp.bfloat16)
            return carry

        lax.fori_loop(0, THIRDS * quads, turn, 0)
        send(0, h)
        keep_own(h).start()
    for h in range(STREAMS):
        absorb(0, h)
        send(1, h)

    def general(r, carry):
        for h in range(STREAMS):
            absorb(r - 1, h)
            for k in range(4):
                remote(r % 2, h, k).wait_send()
            send(r, h)
        return carry

    lax.fori_loop(2, rounds, general, 0)
    for h in range(STREAMS):
        absorb(rounds - 1, h)
        for parity in range(2):
            for k in range(4):
                remote(parity, h, k).wait_send()
    for h in range(STREAMS):
        for i in range(1, bands):
            to_band(h, i).wait_send()
        keep_own(h).wait()
        for r in range(rounds):
            keep(r, h).wait()


def exchange(table, white, count, rounds, ident):
    bands, _, _, freqs, sub, _ = white.shape
    rows = freqs * KROWS
    block = bands * sub
    shape = (THIRDS + 4 * rounds, STREAMS, rows, block)
    any_space = pl.BlockSpec(memory_space=pl.ANY)
    return pl.pallas_call(
        functools.partial(exchange_kernel, count, bands, rounds),
        out_shape=jax.ShapeDtypeStruct(shape, white.dtype),
        in_specs=[
            pl.BlockSpec(memory_space=pltpu.SMEM),
            any_space,
            pl.BlockSpec(memory_space=pltpu.VMEM),
        ],
        out_specs=any_space,
        scratch_shapes=[
            pltpu.VMEM(shape, white.dtype),
            pltpu.VMEM((STREAMS, THIRDS, freqs, block, LANES), white.dtype),
            pltpu.VMEM((2, STREAMS, 4, rows, block), white.dtype),
            pltpu.VMEM((2, STREAMS, 4, rows, block), white.dtype),
            pltpu.SemaphoreType.DMA((2, STREAMS, 4)),
            pltpu.SemaphoreType.DMA((2, STREAMS, 4)),
            pltpu.SemaphoreType.DMA((rounds + 1, STREAMS)),
            pltpu.SemaphoreType.DMA((STREAMS, bands)),
            pltpu.SemaphoreType.DMA((STREAMS, bands)),
            pltpu.SemaphoreType.DMA((STREAMS,)),
        ],
        compiler_params=pltpu.CompilerParams(
            vmem_limit_bytes=EXCHANGE_LIMIT, collective_id=ident, has_side_effects=True
        ),
    )(table, white, jnp.asarray(pick_table()))


def gather_all(white):
    bands, _, _, freqs, sub, _ = white.shape
    banded = white.reshape(bands, THIRDS * STREAMS * freqs, sub, LANES)
    banded = lax.all_to_all(banded, "tm", split_axis=0, concat_axis=0, tiled=True)
    own = compact(banded).reshape(THIRDS, STREAMS, freqs * KROWS, bands * sub)
    return lax.all_gather(own, "chan", axis=0, tiled=True)


def cross_spectra(table, slot_of, rounds, white, blocks, live, count):
    thirds = jnp.arange(THIRDS, dtype=jnp.int32)[None, :]

    def by_rounds(choice, ident):
        def run():
            held = exchange(table, white, count, choice, ident)
            return products(held, slot_of[blocks[:, None] + count * thirds], live)

        return run

    def whole():
        return products(gather_all(white), blocks[:, None] * THIRDS + thirds, live)

    branches = [by_rounds(choice, i) for i, choice in enumerate(ROUND_CHOICES)] + [whole]
    which = sum((rounds > choice).astype(jnp.int32) for choice in ROUND_CHOICES)
    return lax.switch(which, branches)


def product_kernel(needed_ref, live_ref, left_ref, right_ref, out_ref):
    slot = pl.program_id(0)
    streams, rows, block = left_ref.shape[1:]
    norm = 1.0 / math.sqrt(SEG)
    dims = (((0,), (0,)), ((), ()))
    per = rows // (QUAD * KROWS)

    @pl.when(live_ref[slot] != 0)
    def _():
        def one(g, carry):
            at = pl.ds(pl.multiple_of(g % per * (QUAD * KROWS), 16), QUAD * KROWS)
            left4 = left_ref[0, g // per, at]
            right4 = right_ref[0, g // per, at]
            for q in range(QUAD):
                left = left4[q * KROWS : (q + 1) * KROWS]
                right = right4[q * KROWS : (q + 1) * KROWS]
                turned = jnp.concatenate([-right[SEG:], right[:SEG]], axis=0)
                both = jnp.concatenate([right, turned], axis=1)
                value = lax.dot_general(left, both, dims, preferred_element_type=jnp.float32)
                value = (value * norm).astype(jnp.bfloat16)
                out_ref[0, g * QUAD + q, 0] = value[:, :block]
                out_ref[0, g * QUAD + q, 1] = value[:, block:]
            return carry

        lax.fori_loop(0, streams * per, one, 0)

    @pl.when(live_ref[slot] == 0)
    def _():
        out_ref[...] = jnp.zeros_like(out_ref)


def products(held, needed, live):
    _, streams, rows, block = held.shape
    part = streams * (rows // KROWS)
    spec = (1, streams, rows, block)
    return pl.pallas_call(
        product_kernel,
        out_shape=jax.ShapeDtypeStruct((PMAX, THIRDS * part, 2, block, block), jnp.bfloat16),
        grid_spec=pltpu.PrefetchScalarGridSpec(
            num_scalar_prefetch=2,
            grid=(PMAX, THIRDS),
            in_specs=[
                pl.BlockSpec(spec, lambda s, g, need, live: (need[2 * s, g], 0, 0, 0)),
                pl.BlockSpec(spec, lambda s, g, need, live: (need[2 * s + 1, g], 0, 0, 0)),
            ],
            out_specs=pl.BlockSpec((1, part, 2, block, block), lambda s, g, need, live: (s, g, 0, 0, 0)),
        ),
        compiler_params=pltpu.CompilerParams(vmem_limit_bytes=PRODUCT_LIMIT),
    )(needed, live, held, held)


def body(records, pairs, owners, starts):
    tm_count = lax.axis_size("tm")
    chan_count = lax.axis_size("chan")
    chans, samp_dev = records.shape
    block = chans // chan_count
    sub = block // tm_count
    group_freq = NFREQ // tm_count
    table, slots, rounds = plan(pairs, owners, chan_count)
    moved = (records * SCALE).astype(jnp.float16).reshape(chan_count * tm_count, sub, samp_dev)
    received = lax.all_to_all(moved, ("chan", "tm"), split_axis=0, concat_axis=0, tiled=True)
    white = spectra(starts, received.astype(jnp.float32), chan_count, tm_count)
    white = white.reshape(tm_count, THIRDS, STREAMS, group_freq // (THIRDS * STREAMS), sub, LANES)
    me_chan = lax.axis_index("chan")
    pair_id, live = slot_table(owners, chan_count)
    mine = lax.dynamic_slice_in_dim(pair_id, me_chan * PMAX, PMAX)
    my_live = lax.dynamic_slice_in_dim(live, me_chan * PMAX, PMAX).astype(jnp.int32)
    blocks = pairs[mine].reshape(2 * PMAX)
    slot_of = lax.dynamic_index_in_dim(slots, me_chan, 0, keepdims=False)
    return cross_spectra(table, slot_of, rounds[0, 0], white, blocks, my_live, chan_count)


def solution(mesh):
    return jax.shard_map(
        body,
        mesh=mesh,
        in_specs=(P(None, ("tm", "chan")), P(), P(), P()),
        out_specs=P("chan", "tm", None, None, None),
        check_vma=False,
    )
```

```python
import functools
import math
import jax
import jax.numpy as jnp
import ml_dtypes
import numpy as np
from jax import lax
from jax.experimental import pallas as pl
from jax.experimental.pallas import tpu as pltpu
from jax.sharding import PartitionSpec as P

NFFT = 1024
NFREQ = 384
WBAND = 64
SEG = 58
SEGP = 64
PMAX = 6
LANES = 128
KROWS = 2 * SEG
QUAD = 4
VMEM_LIMIT = 56 * 1024 * 1024
EXCHANGE_LIMIT = 28 * 1024 * 1024
PRODUCT_LIMIT = 12 * 1024 * 1024
THIRDS = 3
STREAMS = 2
MAX_ROUNDS = 32
ROUND_CHOICES = (7, 8, 9)
RULES = (3, 7)
SCALE = 8192.0


def windowed_table():
    sample = np.arange(NFFT)
    freq = np.arange(NFREQ)
    angle = 2.0 * np.pi * ((freq[:, None] * sample[None, :]) % NFFT) / NFFT
    window = 0.5 - 0.5 * np.cos(2.0 * np.pi * sample / NFFT)
    table = np.concatenate([np.cos(angle), -np.sin(angle)], axis=0) * window[None, :] / SCALE
    high = table.astype(np.float32).astype(ml_dtypes.bfloat16)
    low = (table - high.astype(np.float64)).astype(np.float32).astype(ml_dtypes.bfloat16)
    return high, low


def pick_table():
    pick = np.zeros((QUAD * KROWS, QUAD * LANES), np.float32)
    for q in range(QUAD):
        for part in range(2):
            for s in range(SEG):
                pick[q * KROWS + part * SEG + s, q * LANES + part * SEGP + s] = 1.0
    return pick.astype(ml_dtypes.bfloat16)


def slot_table(owners, owner_count):
    owner = owners[:, 0]
    npair = owner.shape[0]
    order = jnp.arange(npair, dtype=jnp.int32)
    same = owner[:, None] == owner[None, :]
    before = order[None, :] < order[:, None]
    rank = jnp.sum((same & before).astype(jnp.int32), axis=1)
    target = owner * PMAX + rank
    rows = jnp.arange(owner_count * PMAX, dtype=jnp.int32)
    match = target[None, :] == rows[:, None]
    live = jnp.any(match, axis=1)
    pair_id = jnp.sum(jnp.where(match, order[None, :], 0), axis=1)
    return (pair_id, live)


def bits(size):
    assert size & (size - 1) == 0
    return size.bit_length() - 1


def spectra_kernel(
    chan_count, tm_count, starts_ref, rec_ref, high_hbm, low_hbm, out_ref, high_ref, low_ref, frames, spread, sems
):
    fetch = [
        pltpu.make_async_copy(high_hbm, high_ref, sems.at[0]),
        pltpu.make_async_copy(low_hbm, low_ref, sems.at[1]),
    ]
    for copy in fetch:
        copy.start()
    sub = rec_ref.shape[1]
    tiles = rec_ref.shape[2] // LANES
    total_tiles = rec_ref.shape[0] * tiles
    width = NFFT // LANES
    lane = lax.broadcasted_iota(jnp.int32, (sub, LANES), 1)
    for c in range(sub):
        frames[:, c * SEGP + SEG : (c + 1) * SEGP, :] = jnp.zeros(
            (width, SEGP - SEG, LANES), jnp.float32
        )

    def cut(s, carry):
        begin = starts_ref[s]
        base = jnp.minimum(begin >> bits(LANES), total_tiles - width - 1)
        over = begin - base * LANES
        shift = (LANES - over) & (LANES - 1)
        turned = []
        for j in range(width + 1):
            tile = base + j
            piece = tile >> bits(tiles)
            source = (piece & (chan_count - 1)) * tm_count + (piece >> bits(chan_count))
            at = pl.multiple_of((tile & (tiles - 1)) * LANES, LANES)
            turned.append(pltpu.roll(rec_ref[source, :, pl.ds(at, LANES)], shift, 1))
        keep = lane < LANES - over
        for j in range(width):
            frames[j, pl.ds(s, sub, stride=SEGP), :] = jnp.where(keep, turned[j], turned[j + 1])
        return carry

    lax.fori_loop(0, SEG // 4 * 4, cut, 0, unroll=4)
    for s in range(SEG // 4 * 4, SEG):
        cut(s, 0)
    for copy in fetch:
        copy.wait()

    group = 4
    cols = group * SEGP
    dims = (((1,), (1,)), ((), ()))
    half = lax.broadcasted_iota(jnp.int32, (NFREQ, LANES), 1) < SEGP

    def transform(g, carry):
        at = pl.ds(pl.multiple_of(g * cols, cols), cols)
        rows = jnp.concatenate([frames[j, at, :] for j in range(width)], axis=1)
        top = rows.astype(jnp.bfloat16)
        rest = (rows - top.astype(jnp.float32)).astype(jnp.bfloat16)
        parts = []
        for p in range(2):
            hi = high_ref[p * NFREQ : (p + 1) * NFREQ, :]
            lo = low_ref[p * NFREQ : (p + 1) * NFREQ, :]
            value = lax.dot_general(hi, rest, dims, preferred_element_type=jnp.float32)
            value += lax.dot_general(lo, top, dims, preferred_element_type=jnp.float32)
            value += lax.dot_general(hi, top, dims, preferred_element_type=jnp.float32)
            parts.append(value)
        re, im = parts
        power = re * re + im * im
        band = jnp.mean(power.reshape(NFREQ // WBAND, WBAND, cols), axis=1, keepdims=True)
        scale = 1.0 / jnp.sqrt(band + 1e-06)
        scale = jnp.broadcast_to(scale, (NFREQ // WBAND, WBAND, cols)).reshape(NFREQ, cols)
        re = re * scale
        im = im * scale
        for h in range(group // 2):
            a = re[:, h * LANES : (h + 1) * LANES]
            b = im[:, h * LANES : (h + 1) * LANES]
            c = g * group + 2 * h
            even = pl.multiple_of(c * NFREQ, NFREQ)
            spread[pl.ds(even, NFREQ), :] = jnp.where(half, a, pltpu.roll(b, SEGP, 1))
            odd = pl.multiple_of((c + 1) * NFREQ, NFREQ)
            spread[pl.ds(odd, NFREQ), :] = jnp.where(half, pltpu.roll(a, SEGP, 1), b)
        return carry

    lax.fori_loop(0, sub // group, transform, 0, unroll=2)

    def regroup(f, carry):
        for u in range(8):
            k = f * 8 + u
            out_ref[k] = spread[pl.ds(k, sub, stride=NFREQ), :].astype(jnp.bfloat16)
        return carry

    lax.fori_loop(0, NFREQ // 8, regroup, 0, unroll=4)


def spectra(starts, received, chan_count, tm_count):
    sub = received.shape[1]
    high, low = windowed_table()
    vmem = pl.BlockSpec(memory_space=pltpu.VMEM)
    return pl.pallas_call(
        functools.partial(spectra_kernel, chan_count, tm_count),
        out_shape=jax.ShapeDtypeStruct((NFREQ, sub, LANES), jnp.bfloat16),
        in_specs=[
            pl.BlockSpec(memory_space=pltpu.SMEM),
            vmem,
            pl.BlockSpec(memory_space=pl.ANY),
            pl.BlockSpec(memory_space=pl.ANY),
        ],
        out_specs=vmem,
        scratch_shapes=[
            pltpu.VMEM(high.shape, high.dtype),
            pltpu.VMEM(low.shape, low.dtype),
            pltpu.VMEM((NFFT // LANES, sub * SEGP, LANES), jnp.float32),
            pltpu.VMEM((sub * NFREQ, LANES), jnp.float32),
            pltpu.SemaphoreType.DMA((2,)),
        ],
        compiler_params=pltpu.CompilerParams(vmem_limit_bytes=VMEM_LIMIT),
    )(starts, received, jnp.asarray(high), jnp.asarray(low))


def compact_kernel(in_ref, pick_ref, out_ref):
    pieces, freqs, sub, _ = in_ref.shape
    block = pieces * sub
    dims = (((1,), (1,)), ((), ()))

    def one(g, carry):
        wide = jnp.concatenate(
            [
                jnp.concatenate([in_ref[p, g * QUAD + q] for p in range(pieces)], axis=0)
                for q in range(QUAD)
            ],
            axis=1,
        )
        value = lax.dot_general(pick_ref[...], wide, dims, preferred_element_type=jnp.float32)
        out_ref[g] = value.astype(jnp.bfloat16)
        return carry

    lax.fori_loop(0, freqs // QUAD, one, 0)


def compact(banded):
    pieces, freqs, sub, _ = banded.shape
    vmem = pl.BlockSpec(memory_space=pltpu.VMEM)
    return pl.pallas_call(
        compact_kernel,
        out_shape=jax.ShapeDtypeStruct((freqs // QUAD, QUAD * KROWS, pieces * sub), jnp.bfloat16),
        in_specs=[vmem, vmem],
        out_specs=vmem,
        compiler_params=pltpu.CompilerParams(vmem_limit_bytes=VMEM_LIMIT),
    )(banded, jnp.asarray(pick_table()))


def torus_tables(count):
    side = math.isqrt(count)
    index = np.arange(count)
    x, y = index // side, index % side
    sources = [
        (x + 1) % side * side + y,
        (x - 1) % side * side + y,
        x * side + (y + 1) % side,
        x * side + (y - 1) % side,
    ]
    every = np.eye(len(RULES))
    near = np.concatenate([np.kron(every, np.eye(count)[source]) for source in sources], axis=0)
    dx = np.abs(x[:, None] - x[None, :])
    dy = np.abs(y[:, None] - y[None, :])
    dist = np.minimum(dx, side - dx) + np.minimum(dy, side - dy)
    reach = np.concatenate([np.kron(every, dist <= d) for d in range(4)], axis=0)
    shell = np.concatenate([np.kron(every, (dist == d) * 2.0 ** (3 - d)) for d in range(4)], axis=1)
    return [t.astype(ml_dtypes.bfloat16) for t in (near, reach, shell)]


def plan_kernel(pairs_ref, owners_ref, near_ref, reach_ref, shell_ref, table_ref, slots_ref, rounds_ref):
    rows = near_ref.shape[1]
    count = rows // len(RULES)
    shape = (rows, LANES)
    row = lax.broadcasted_iota(jnp.int32, shape, 0)
    node = row % count
    turn = jnp.where(row < count, RULES[0], RULES[1])
    lane = lax.broadcasted_iota(jnp.int32, shape, 1)
    inside = lane < THIRDS * count
    block = lane % count
    third = lane // count
    commodities = THIRDS * count
    tie = commodities - 1 - (lane + turn * node) % commodities
    tie = jnp.where(inside, tie, 0).astype(jnp.float32)

    def mark(p, need):
        hit = (block == pairs_ref[p, 0]) | (block == pairs_ref[p, 1])
        return jnp.where(hit & (node == owners_ref[p, 0]) & inside, 1.0, need)

    need = lax.fori_loop(0, pairs_ref.shape[0], mark, jnp.zeros(shape, jnp.float32))
    has = jnp.where((block == node) & inside, 1.0, 0.0)
    slot_of = jnp.where(has > 0, third, 0).astype(jnp.float32)
    table = jnp.zeros(shape, jnp.float32)

    def dot(m, v):
        return jnp.dot(m, v.astype(jnp.bfloat16), preferred_element_type=jnp.float32)

    def unfinished(state):
        r, left, _, _, _ = state
        return (left > 0) & (r < MAX_ROUNDS)

    def one(state):
        r, _, has, slot_of, table = state
        rem = need * (1.0 - has)
        short = rem * jnp.sum(rem, axis=1, keepdims=True)
        reached = dot(reach_ref[...], has)
        waves = jnp.concatenate(
            [jnp.where(reached[d * rows : (d + 1) * rows] > 0, 0.0, short) for d in range(4)], axis=0
        )
        gain = dot(shell_ref[...], waves)
        both = dot(near_ref[...], jnp.concatenate([has, slot_of], axis=1))
        near_has = [both[k * rows : (k + 1) * rows, :LANES] for k in range(4)]
        near_slot = [both[k * rows : (k + 1) * rows, LANES:] for k in range(4)]
        sources = near_has[0] + near_has[1] + near_has[2] + near_has[3]
        scarce = 5.0 - sources
        worth = jnp.where((gain > 0) & (has == 0), gain * scarce * scarce * 64.0 + tie, 0.0)
        for k in range(4):
            key = worth * near_has[k]
            best = jnp.max(key, axis=1, keepdims=True)
            chosen = (key == best) & (key > 0)
            worth = jnp.where(chosen, 0.0, worth)
            has = jnp.where(chosen, 1.0, has)
            source = jnp.sum(jnp.where(chosen, near_slot[k], 0.0), axis=1, keepdims=True)
            table = jnp.where(lane == 4 * r + k, source, table)
            slot_of = jnp.where(chosen, (THIRDS + 4 * r + k).astype(jnp.float32), slot_of)
        return r + 1, jnp.minimum(*missing(has)), has, slot_of, table

    def missing(has):
        rem = need * (1.0 - has)
        return jnp.sum(rem[:count]), jnp.sum(rem[count:])

    rounds, left, has, slot_of, table = lax.while_loop(
        unfinished, one, (jnp.int32(0), jnp.float32(1.0), has, slot_of, table)
    )
    first = missing(has)[0] == 0
    table_ref[...] = jnp.where(first, table[:count], table[count:]).astype(jnp.int32)
    slots_ref[...] = jnp.where(first, slot_of[:count], slot_of[count:]).astype(jnp.int32)
    rounds_ref[...] = jnp.full(rounds_ref.shape, jnp.where(left > 0, MAX_ROUNDS, rounds), jnp.int32)


def plan(pairs, owners, count):
    near, reach, shell = torus_tables(count)
    vmem = pl.BlockSpec(memory_space=pltpu.VMEM)
    smem = pl.BlockSpec(memory_space=pltpu.SMEM)
    grid = jax.ShapeDtypeStruct((count, LANES), jnp.int32)
    return pl.pallas_call(
        plan_kernel,
        out_shape=(grid, grid, jax.ShapeDtypeStruct((8, LANES), jnp.int32)),
        in_specs=[smem, smem, vmem, vmem, vmem],
        out_specs=(vmem, vmem, vmem),
    )(pairs, owners, jnp.asarray(near), jnp.asarray(reach), jnp.asarray(shell))


def exchange_kernel(
    count,
    bands,
    rounds,
    table_ref,
    white_ref,
    pick_ref,
    out_ref,
    held,
    spread,
    land,
    stage,
    send_sem,
    recv_sem,
    out_sem,
    band_send,
    band_recv,
    band_own,
):
    side = math.isqrt(count)
    me = lax.axis_index("chan")
    x, y = me // side, me % side
    targets = [
        (x + side - 1) % side * side + y,
        (x + 1) % side * side + y,
        x * side + (y + side - 1) % side,
        x * side + (y + 1) % side,
    ]
    rows = held.shape[2]
    sub = white_ref.shape[4]
    step = 32
    band = lax.axis_index("tm")

    barrier = pltpu.get_barrier_semaphore()
    for k in range(4):
        pl.semaphore_signal(
            barrier, inc=1, device_id={"chan": targets[k]}, device_id_type=pl.DeviceIdType.MESH
        )
    for i in range(1, bands):
        pl.semaphore_signal(
            barrier, inc=1, device_id={"tm": (band + i) % bands}, device_id_type=pl.DeviceIdType.MESH
        )
    pl.semaphore_wait(barrier, 4 + bands - 1)

    def place(source):
        return pl.ds(pl.multiple_of(source * sub, sub), sub)

    def to_band(h, i):
        target = (band + i) % bands
        return pltpu.make_async_remote_copy(
            src_ref=white_ref.at[target, :, h],
            dst_ref=spread.at[h, :, :, place(band)],
            send_sem=band_send.at[h, i],
            recv_sem=band_recv.at[h, i],
            device_id={"tm": target},
            device_id_type=pl.DeviceIdType.MESH,
        )

    def from_band(h, i):
        source = (band + bands - i) % bands
        return pltpu.make_async_remote_copy(
            src_ref=white_ref.at[source, :, h],
            dst_ref=spread.at[h, :, :, place(source)],
            send_sem=band_send.at[h, i],
            recv_sem=band_recv.at[h, i],
            device_id={"tm": source},
            device_id_type=pl.DeviceIdType.MESH,
        )

    def stay(h):
        return pltpu.make_async_copy(
            white_ref.at[band, :, h], spread.at[h, :, :, place(band)], band_own.at[h]
        )

    for h in range(STREAMS):
        for i in range(1, bands):
            to_band(h, i).start()
        stay(h).start()

    def each_chunk(work):
        def run(i, carry):
            work(pl.ds(pl.multiple_of(i * step, step), step))
            return carry

        lax.fori_loop(0, rows // step, run, 0)

    def remote(parity, h, k):
        return pltpu.make_async_remote_copy(
            src_ref=stage.at[parity, h, k],
            dst_ref=land.at[parity, h, k],
            send_sem=send_sem.at[parity, h, k],
            recv_sem=recv_sem.at[parity, h, k],
            device_id={"chan": targets[k]},
            device_id_type=pl.DeviceIdType.MESH,
        )

    def keep_own(h):
        return pltpu.make_async_copy(
            held.at[pl.ds(0, THIRDS), h], out_ref.at[pl.ds(0, THIRDS), h], out_sem.at[rounds, h]
        )

    def keep(r, h):
        at = pl.ds(THIRDS + 4 * r, 4)
        return pltpu.make_async_copy(held.at[at, h], out_ref.at[at, h], out_sem.at[r, h])

    def absorb(r, h):
        parity = r % 2
        for k in range(4):
            remote(parity, h, k).wait_recv()

        def work(at):
            for k in range(4):
                held[THIRDS + 4 * r + k, h, at, :] = land[parity, h, k, at, :]

        each_chunk(work)
        keep(r, h).start()

    def send(r, h):
        parity = r % 2
        source = [table_ref[targets[k], 4 * r + k] for k in range(4)]

        def work(at):
            for k in range(4):
                stage[parity, h, k, at, :] = held[source[k], h, at, :]

        each_chunk(work)
        for k in range(4):
            remote(parity, h, k).start()

    dims = (((1,), (1,)), ((), ()))
    quads = spread.shape[2] // QUAD

    for h in range(STREAMS):
        stay(h).wait()
        for i in range(1, bands):
            from_band(h, i).wait_recv()

        def turn(g, carry):
            s, part = g // quads, g % quads
            wide = jnp.concatenate([spread[h, s, part * QUAD + q] for q in range(QUAD)], axis=1)
            value = lax.dot_general(pick_ref[...], wide, dims, preferred_element_type=jnp.float32)
            at = pl.ds(pl.multiple_of(part * (QUAD * KROWS), QUAD * KROWS), QUAD * KROWS)
            held[s, h, at, :] = value.astype(jnp.bfloat16)
            return carry

        lax.fori_loop(0, THIRDS * quads, turn, 0)
        send(0, h)
        keep_own(h).start()
    for h in range(STREAMS):
        absorb(0, h)
        send(1, h)

    def general(r, carry):
        for h in range(STREAMS):
            absorb(r - 1, h)
            for k in range(4):
                remote(r % 2, h, k).wait_send()
            send(r, h)
        return carry

    lax.fori_loop(2, rounds, general, 0)
    for h in range(STREAMS):
        absorb(rounds - 1, h)
        for parity in range(2):
            for k in range(4):
                remote(parity, h, k).wait_send()
    for h in range(STREAMS):
        for i in range(1, bands):
            to_band(h, i).wait_send()
        keep_own(h).wait()
        for r in range(rounds):
            keep(r, h).wait()


def exchange(table, white, count, rounds, ident):
    bands, _, _, freqs, sub, _ = white.shape
    rows = freqs * KROWS
    block = bands * sub
    shape = (THIRDS + 4 * rounds, STREAMS, rows, block)
    any_space = pl.BlockSpec(memory_space=pl.ANY)
    return pl.pallas_call(
        functools.partial(exchange_kernel, count, bands, rounds),
        out_shape=jax.ShapeDtypeStruct(shape, white.dtype),
        in_specs=[
            pl.BlockSpec(memory_space=pltpu.SMEM),
            any_space,
            pl.BlockSpec(memory_space=pltpu.VMEM),
        ],
        out_specs=any_space,
        scratch_shapes=[
            pltpu.VMEM(shape, white.dtype),
            pltpu.VMEM((STREAMS, THIRDS, freqs, block, LANES), white.dtype),
            pltpu.VMEM((2, STREAMS, 4, rows, block), white.dtype),
            pltpu.VMEM((2, STREAMS, 4, rows, block), white.dtype),
            pltpu.SemaphoreType.DMA((2, STREAMS, 4)),
            pltpu.SemaphoreType.DMA((2, STREAMS, 4)),
            pltpu.SemaphoreType.DMA((rounds + 1, STREAMS)),
            pltpu.SemaphoreType.DMA((STREAMS, bands)),
            pltpu.SemaphoreType.DMA((STREAMS, bands)),
            pltpu.SemaphoreType.DMA((STREAMS,)),
        ],
        compiler_params=pltpu.CompilerParams(
            vmem_limit_bytes=EXCHANGE_LIMIT, collective_id=ident, has_side_effects=True
        ),
    )(table, white, jnp.asarray(pick_table()))


def gather_all(white):
    bands, _, _, freqs, sub, _ = white.shape
    banded = white.reshape(bands, THIRDS * STREAMS * freqs, sub, LANES)
    banded = lax.all_to_all(banded, "tm", split_axis=0, concat_axis=0, tiled=True)
    own = compact(banded).reshape(THIRDS, STREAMS, freqs * KROWS, bands * sub)
    return lax.all_gather(own, "chan", axis=0, tiled=True)


def cross_spectra(table, slot_of, rounds, white, blocks, live, count):
    thirds = jnp.arange(THIRDS, dtype=jnp.int32)[None, :]

    def by_rounds(choice, ident):
        def run():
            held = exchange(table, white, count, choice, ident)
            return products(held, slot_of[blocks[:, None] + count * thirds], live)

        return run

    def whole():
        return products(gather_all(white), blocks[:, None] * THIRDS + thirds, live)

    branches = [by_rounds(choice, i) for i, choice in enumerate(ROUND_CHOICES)] + [whole]
    which = sum((rounds > choice).astype(jnp.int32) for choice in ROUND_CHOICES)
    return lax.switch(which, branches)


def product_kernel(needed_ref, live_ref, left_ref, right_ref, out_ref):
    slot = pl.program_id(0)
    streams, rows, block = left_ref.shape[1:]
    norm = 1.0 / math.sqrt(SEG)
    dims = (((0,), (0,)), ((), ()))
    per = rows // (QUAD * KROWS)

    @pl.when(live_ref[slot] != 0)
    def _():
        def one(g, carry):
            at = pl.ds(pl.multiple_of(g % per * (QUAD * KROWS), 16), QUAD * KROWS)
            left4 = left_ref[0, g // per, at]
            right4 = right_ref[0, g // per, at]
            for q in range(QUAD):
                left = left4[q * KROWS : (q + 1) * KROWS]
                right = right4[q * KROWS : (q + 1) * KROWS]
                turned = jnp.concatenate([-right[SEG:], right[:SEG]], axis=0)
                both = jnp.concatenate([right, turned], axis=1)
                value = lax.dot_general(left, both, dims, preferred_element_type=jnp.float32)
                value = (value * norm).astype(jnp.bfloat16)
                out_ref[0, g * QUAD + q, 0] = value[:, :block]
                out_ref[0, g * QUAD + q, 1] = value[:, block:]
            return carry

        lax.fori_loop(0, streams * per, one, 0, unroll=True)

    @pl.when(live_ref[slot] == 0)
    def _():
        out_ref[...] = jnp.zeros_like(out_ref)


def products(held, needed, live):
    _, streams, rows, block = held.shape
    part = streams * (rows // KROWS)
    spec = (1, streams, rows, block)
    return pl.pallas_call(
        product_kernel,
        out_shape=jax.ShapeDtypeStruct((PMAX, THIRDS * part, 2, block, block), jnp.bfloat16),
        grid_spec=pltpu.PrefetchScalarGridSpec(
            num_scalar_prefetch=2,
            grid=(PMAX, THIRDS),
            in_specs=[
                pl.BlockSpec(spec, lambda s, g, need, live: (need[2 * s, g], 0, 0, 0)),
                pl.BlockSpec(spec, lambda s, g, need, live: (need[2 * s + 1, g], 0, 0, 0)),
            ],
            out_specs=pl.BlockSpec((1, part, 2, block, block), lambda s, g, need, live: (s, g, 0, 0, 0)),
        ),
        compiler_params=pltpu.CompilerParams(vmem_limit_bytes=PRODUCT_LIMIT),
    )(needed, live, held, held)


def body(records, pairs, owners, starts):
    tm_count = lax.axis_size("tm")
    chan_count = lax.axis_size("chan")
    chans, samp_dev = records.shape
    block = chans // chan_count
    sub = block // tm_count
    group_freq = NFREQ // tm_count
    table, slots, rounds = plan(pairs, owners, chan_count)
    moved = (records * SCALE).astype(jnp.float16).reshape(chan_count * tm_count, sub, samp_dev)
    received = lax.all_to_all(moved, ("chan", "tm"), split_axis=0, concat_axis=0, tiled=True)
    white = spectra(starts, received.astype(jnp.float32), chan_count, tm_count)
    white = white.reshape(tm_count, THIRDS, STREAMS, group_freq // (THIRDS * STREAMS), sub, LANES)
    me_chan = lax.axis_index("chan")
    pair_id, live = slot_table(owners, chan_count)
    mine = lax.dynamic_slice_in_dim(pair_id, me_chan * PMAX, PMAX)
    my_live = lax.dynamic_slice_in_dim(live, me_chan * PMAX, PMAX).astype(jnp.int32)
    blocks = pairs[mine].reshape(2 * PMAX)
    slot_of = lax.dynamic_index_in_dim(slots, me_chan, 0, keepdims=False)
    return cross_spectra(table, slot_of, rounds[0, 0], white, blocks, my_live, chan_count)


def solution(mesh):
    return jax.shard_map(
        body,
        mesh=mesh,
        in_specs=(P(None, ("tm", "chan")), P(), P(), P()),
        out_specs=P("chan", "tm", None, None, None),
        check_vma=False,
    )
```

```python
import functools
import math
import jax
import jax.numpy as jnp
import ml_dtypes
import numpy as np
from jax import lax
from jax.experimental import pallas as pl
from jax.experimental.pallas import tpu as pltpu
from jax.sharding import PartitionSpec as P

NFFT = 1024
NFREQ = 384
WBAND = 64
SEG = 58
SEGP = 64
PMAX = 6
LANES = 128
KROWS = 2 * SEG
QUAD = 4
VMEM_LIMIT = 56 * 1024 * 1024
EXCHANGE_LIMIT = 28 * 1024 * 1024
PRODUCT_LIMIT = 12 * 1024 * 1024
THIRDS = 3
STREAMS = 4
DELAYS = (0, 0, 1, 1)
LEAD = 2
MAX_ROUNDS = 32
ROUND_CHOICES = (7, 8, 9)
RULES = (3, 7)
SCALE = 8192.0


def windowed_table():
    sample = np.arange(NFFT)
    freq = np.arange(NFREQ)
    angle = 2.0 * np.pi * ((freq[:, None] * sample[None, :]) % NFFT) / NFFT
    window = 0.5 - 0.5 * np.cos(2.0 * np.pi * sample / NFFT)
    table = np.concatenate([np.cos(angle), -np.sin(angle)], axis=0) * window[None, :] / SCALE
    high = table.astype(np.float32).astype(ml_dtypes.bfloat16)
    low = (table - high.astype(np.float64)).astype(np.float32).astype(ml_dtypes.bfloat16)
    return high, low


def pick_table():
    pick = np.zeros((QUAD * KROWS, QUAD * LANES), np.float32)
    for q in range(QUAD):
        for part in range(2):
            for s in range(SEG):
                pick[q * KROWS + part * SEG + s, q * LANES + part * SEGP + s] = 1.0
    return pick.astype(ml_dtypes.bfloat16)


def slot_table(owners, owner_count):
    owner = owners[:, 0]
    npair = owner.shape[0]
    order = jnp.arange(npair, dtype=jnp.int32)
    same = owner[:, None] == owner[None, :]
    before = order[None, :] < order[:, None]
    rank = jnp.sum((same & before).astype(jnp.int32), axis=1)
    target = owner * PMAX + rank
    rows = jnp.arange(owner_count * PMAX, dtype=jnp.int32)
    match = target[None, :] == rows[:, None]
    live = jnp.any(match, axis=1)
    pair_id = jnp.sum(jnp.where(match, order[None, :], 0), axis=1)
    return (pair_id, live)


def bits(size):
    assert size & (size - 1) == 0
    return size.bit_length() - 1


def spectra_kernel(
    chan_count, tm_count, starts_ref, rec_ref, high_hbm, low_hbm, out_ref, high_ref, low_ref, frames, spread, sems
):
    fetch = [
        pltpu.make_async_copy(high_hbm, high_ref, sems.at[0]),
        pltpu.make_async_copy(low_hbm, low_ref, sems.at[1]),
    ]
    for copy in fetch:
        copy.start()
    sub = rec_ref.shape[1]
    tiles = rec_ref.shape[2] // LANES
    total_tiles = rec_ref.shape[0] * tiles
    width = NFFT // LANES
    lane = lax.broadcasted_iota(jnp.int32, (sub, LANES), 1)
    for c in range(sub):
        frames[:, c * SEGP + SEG : (c + 1) * SEGP, :] = jnp.zeros(
            (width, SEGP - SEG, LANES), jnp.float32
        )

    def cut(s, carry):
        begin = starts_ref[s]
        base = jnp.minimum(begin >> bits(LANES), total_tiles - width - 1)
        over = begin - base * LANES
        shift = (LANES - over) & (LANES - 1)
        turned = []
        for j in range(width + 1):
            tile = base + j
            piece = tile >> bits(tiles)
            source = (piece & (chan_count - 1)) * tm_count + (piece >> bits(chan_count))
            at = pl.multiple_of((tile & (tiles - 1)) * LANES, LANES)
            turned.append(pltpu.roll(rec_ref[source, :, pl.ds(at, LANES)], shift, 1))
        keep = lane < LANES - over
        for j in range(width):
            frames[j, pl.ds(s, sub, stride=SEGP), :] = jnp.where(keep, turned[j], turned[j + 1])
        return carry

    lax.fori_loop(0, SEG // 4 * 4, cut, 0, unroll=4)
    for s in range(SEG // 4 * 4, SEG):
        cut(s, 0)
    for copy in fetch:
        copy.wait()

    group = 4
    cols = group * SEGP
    dims = (((1,), (1,)), ((), ()))
    half = lax.broadcasted_iota(jnp.int32, (NFREQ, LANES), 1) < SEGP

    def transform(g, carry):
        at = pl.ds(pl.multiple_of(g * cols, cols), cols)
        rows = jnp.concatenate([frames[j, at, :] for j in range(width)], axis=1)
        top = rows.astype(jnp.bfloat16)
        rest = (rows - top.astype(jnp.float32)).astype(jnp.bfloat16)
        parts = []
        for p in range(2):
            hi = high_ref[p * NFREQ : (p + 1) * NFREQ, :]
            lo = low_ref[p * NFREQ : (p + 1) * NFREQ, :]
            value = lax.dot_general(hi, rest, dims, preferred_element_type=jnp.float32)
            value += lax.dot_general(lo, top, dims, preferred_element_type=jnp.float32)
            value += lax.dot_general(hi, top, dims, preferred_element_type=jnp.float32)
            parts.append(value)
        re, im = parts
        power = re * re + im * im
        band = jnp.mean(power.reshape(NFREQ // WBAND, WBAND, cols), axis=1, keepdims=True)
        scale = 1.0 / jnp.sqrt(band + 1e-06)
        scale = jnp.broadcast_to(scale, (NFREQ // WBAND, WBAND, cols)).reshape(NFREQ, cols)
        re = re * scale
        im = im * scale
        for h in range(group // 2):
            a = re[:, h * LANES : (h + 1) * LANES]
            b = im[:, h * LANES : (h + 1) * LANES]
            c = g * group + 2 * h
            even = pl.multiple_of(c * NFREQ, NFREQ)
            spread[pl.ds(even, NFREQ), :] = jnp.where(half, a, pltpu.roll(b, SEGP, 1))
            odd = pl.multiple_of((c + 1) * NFREQ, NFREQ)
            spread[pl.ds(odd, NFREQ), :] = jnp.where(half, pltpu.roll(a, SEGP, 1), b)
        return carry

    lax.fori_loop(0, sub // group, transform, 0, unroll=2)

    def regroup(f, carry):
        for u in range(8):
            k = f * 8 + u
            out_ref[k] = spread[pl.ds(k, sub, stride=NFREQ), :].astype(jnp.bfloat16)
        return carry

    lax.fori_loop(0, NFREQ // 8, regroup, 0, unroll=4)


def spectra(starts, received, chan_count, tm_count):
    sub = received.shape[1]
    high, low = windowed_table()
    vmem = pl.BlockSpec(memory_space=pltpu.VMEM)
    return pl.pallas_call(
        functools.partial(spectra_kernel, chan_count, tm_count),
        out_shape=jax.ShapeDtypeStruct((NFREQ, sub, LANES), jnp.bfloat16),
        in_specs=[
            pl.BlockSpec(memory_space=pltpu.SMEM),
            vmem,
            pl.BlockSpec(memory_space=pl.ANY),
            pl.BlockSpec(memory_space=pl.ANY),
        ],
        out_specs=vmem,
        scratch_shapes=[
            pltpu.VMEM(high.shape, high.dtype),
            pltpu.VMEM(low.shape, low.dtype),
            pltpu.VMEM((NFFT // LANES, sub * SEGP, LANES), jnp.float32),
            pltpu.VMEM((sub * NFREQ, LANES), jnp.float32),
            pltpu.SemaphoreType.DMA((2,)),
        ],
        compiler_params=pltpu.CompilerParams(vmem_limit_bytes=VMEM_LIMIT),
    )(starts, received, jnp.asarray(high), jnp.asarray(low))


def compact_kernel(in_ref, pick_ref, out_ref):
    pieces, freqs, sub, _ = in_ref.shape
    block = pieces * sub
    dims = (((1,), (1,)), ((), ()))

    def one(g, carry):
        wide = jnp.concatenate(
            [
                jnp.concatenate([in_ref[p, g * QUAD + q] for p in range(pieces)], axis=0)
                for q in range(QUAD)
            ],
            axis=1,
        )
        value = lax.dot_general(pick_ref[...], wide, dims, preferred_element_type=jnp.float32)
        out_ref[g] = value.astype(jnp.bfloat16)
        return carry

    lax.fori_loop(0, freqs // QUAD, one, 0)


def compact(banded):
    pieces, freqs, sub, _ = banded.shape
    vmem = pl.BlockSpec(memory_space=pltpu.VMEM)
    return pl.pallas_call(
        compact_kernel,
        out_shape=jax.ShapeDtypeStruct((freqs // QUAD, QUAD * KROWS, pieces * sub), jnp.bfloat16),
        in_specs=[vmem, vmem],
        out_specs=vmem,
        compiler_params=pltpu.CompilerParams(vmem_limit_bytes=VMEM_LIMIT),
    )(banded, jnp.asarray(pick_table()))


def torus_tables(count):
    side = math.isqrt(count)
    index = np.arange(count)
    x, y = index // side, index % side
    sources = [
        (x + 1) % side * side + y,
        (x - 1) % side * side + y,
        x * side + (y + 1) % side,
        x * side + (y - 1) % side,
    ]
    every = np.eye(len(RULES))
    near = np.concatenate([np.kron(every, np.eye(count)[source]) for source in sources], axis=0)
    dx = np.abs(x[:, None] - x[None, :])
    dy = np.abs(y[:, None] - y[None, :])
    dist = np.minimum(dx, side - dx) + np.minimum(dy, side - dy)
    reach = np.concatenate([np.kron(every, dist <= d) for d in range(4)], axis=0)
    shell = np.concatenate([np.kron(every, (dist == d) * 2.0 ** (3 - d)) for d in range(4)], axis=1)
    return [t.astype(ml_dtypes.bfloat16) for t in (near, reach, shell)]


def plan_kernel(pairs_ref, owners_ref, near_ref, reach_ref, shell_ref, table_ref, slots_ref, rounds_ref):
    rows = near_ref.shape[1]
    count = rows // len(RULES)
    shape = (rows, LANES)
    row = lax.broadcasted_iota(jnp.int32, shape, 0)
    node = row % count
    turn = jnp.where(row < count, RULES[0], RULES[1])
    lane = lax.broadcasted_iota(jnp.int32, shape, 1)
    inside = lane < THIRDS * count
    block = lane % count
    third = lane // count
    commodities = THIRDS * count
    tie = commodities - 1 - (lane + turn * node) % commodities
    tie = jnp.where(inside, tie, 0).astype(jnp.float32)

    def mark(p, need):
        hit = (block == pairs_ref[p, 0]) | (block == pairs_ref[p, 1])
        return jnp.where(hit & (node == owners_ref[p, 0]) & inside, 1.0, need)

    need = lax.fori_loop(0, pairs_ref.shape[0], mark, jnp.zeros(shape, jnp.float32))
    has = jnp.where((block == node) & inside, 1.0, 0.0)
    slot_of = jnp.where(has > 0, third, 0).astype(jnp.float32)
    table = jnp.zeros(shape, jnp.float32)

    def dot(m, v):
        return jnp.dot(m, v.astype(jnp.bfloat16), preferred_element_type=jnp.float32)

    def unfinished(state):
        r, left, _, _, _ = state
        return (left > 0) & (r < MAX_ROUNDS)

    def one(state):
        r, _, has, slot_of, table = state
        rem = need * (1.0 - has)
        short = rem * jnp.sum(rem, axis=1, keepdims=True)
        reached = dot(reach_ref[...], has)
        waves = jnp.concatenate(
            [jnp.where(reached[d * rows : (d + 1) * rows] > 0, 0.0, short) for d in range(4)], axis=0
        )
        gain = dot(shell_ref[...], waves)
        both = dot(near_ref[...], jnp.concatenate([has, slot_of], axis=1))
        near_has = [both[k * rows : (k + 1) * rows, :LANES] for k in range(4)]
        near_slot = [both[k * rows : (k + 1) * rows, LANES:] for k in range(4)]
        sources = near_has[0] + near_has[1] + near_has[2] + near_has[3]
        scarce = 5.0 - sources
        worth = jnp.where((gain > 0) & (has == 0), gain * scarce * scarce * 64.0 + tie, 0.0)
        for k in range(4):
            key = worth * near_has[k]
            best = jnp.max(key, axis=1, keepdims=True)
            chosen = (key == best) & (key > 0)
            worth = jnp.where(chosen, 0.0, worth)
            has = jnp.where(chosen, 1.0, has)
            source = jnp.sum(jnp.where(chosen, near_slot[k], 0.0), axis=1, keepdims=True)
            table = jnp.where(lane == 4 * r + k, source, table)
            slot_of = jnp.where(chosen, (THIRDS + 4 * r + k).astype(jnp.float32), slot_of)
        return r + 1, jnp.minimum(*missing(has)), has, slot_of, table

    def missing(has):
        rem = need * (1.0 - has)
        return jnp.sum(rem[:count]), jnp.sum(rem[count:])

    rounds, left, has, slot_of, table = lax.while_loop(
        unfinished, one, (jnp.int32(0), jnp.float32(1.0), has, slot_of, table)
    )
    first = missing(has)[0] == 0
    table_ref[...] = jnp.where(first, table[:count], table[count:]).astype(jnp.int32)
    slots_ref[...] = jnp.where(first, slot_of[:count], slot_of[count:]).astype(jnp.int32)
    rounds_ref[...] = jnp.full(rounds_ref.shape, jnp.where(left > 0, MAX_ROUNDS, rounds), jnp.int32)


def plan(pairs, owners, count):
    near, reach, shell = torus_tables(count)
    vmem = pl.BlockSpec(memory_space=pltpu.VMEM)
    smem = pl.BlockSpec(memory_space=pltpu.SMEM)
    grid = jax.ShapeDtypeStruct((count, LANES), jnp.int32)
    return pl.pallas_call(
        plan_kernel,
        out_shape=(grid, grid, jax.ShapeDtypeStruct((8, LANES), jnp.int32)),
        in_specs=[smem, smem, vmem, vmem, vmem],
        out_specs=(vmem, vmem, vmem),
    )(pairs, owners, jnp.asarray(near), jnp.asarray(reach), jnp.asarray(shell))


def exchange_kernel(
    count,
    bands,
    rounds,
    table_ref,
    white_ref,
    pick_ref,
    out_ref,
    held,
    spread,
    land,
    stage,
    send_sem,
    recv_sem,
    out_sem,
    band_send,
    band_recv,
    band_own,
):
    side = math.isqrt(count)
    me = lax.axis_index("chan")
    x, y = me // side, me % side
    targets = [
        (x + side - 1) % side * side + y,
        (x + 1) % side * side + y,
        x * side + (y + side - 1) % side,
        x * side + (y + 1) % side,
    ]
    rows = held.shape[2]
    sub = white_ref.shape[4]
    step = 16
    band = lax.axis_index("tm")

    barrier = pltpu.get_barrier_semaphore()
    for k in range(4):
        pl.semaphore_signal(
            barrier, inc=1, device_id={"chan": targets[k]}, device_id_type=pl.DeviceIdType.MESH
        )
    for i in range(1, bands):
        pl.semaphore_signal(
            barrier, inc=1, device_id={"tm": (band + i) % bands}, device_id_type=pl.DeviceIdType.MESH
        )
    pl.semaphore_wait(barrier, 4 + bands - 1)

    def place(source):
        return pl.ds(pl.multiple_of(source * sub, sub), sub)

    def band_copy(h, i, source, target, peer):
        return pltpu.make_async_remote_copy(
            src_ref=white_ref.at[target, :, h],
            dst_ref=spread.at[h, :, :, place(source)],
            send_sem=band_send.at[h, i],
            recv_sem=band_recv.at[h, i],
            device_id={"tm": peer},
            device_id_type=pl.DeviceIdType.MESH,
        )

    def to_band(h, i):
        target = (band + i) % bands
        return band_copy(h, i, band, target, target)

    def from_band(h, i):
        source = (band + bands - i) % bands
        return band_copy(h, i, source, source, source)

    def stay(h):
        return pltpu.make_async_copy(
            white_ref.at[band, :, h], spread.at[h, :, :, place(band)], band_own.at[h]
        )

    def spread_out(h):
        for i in range(1, bands):
            to_band(h, i).start()
        stay(h).start()

    def each_chunk(work):
        def run(i, carry):
            work(pl.ds(pl.multiple_of(i * step, step), step))
            return carry

        lax.fori_loop(0, rows // step, run, 0)

    def remote(parity, h, k):
        return pltpu.make_async_remote_copy(
            src_ref=stage.at[parity, h, k],
            dst_ref=land.at[parity, h, k],
            send_sem=send_sem.at[parity, h, k],
            recv_sem=recv_sem.at[parity, h, k],
            device_id={"chan": targets[k]},
            device_id_type=pl.DeviceIdType.MESH,
        )

    def keep_own(h):
        return pltpu.make_async_copy(
            held.at[pl.ds(0, THIRDS), h], out_ref.at[pl.ds(0, THIRDS), h], out_sem.at[rounds, h]
        )

    def keep(r, h):
        at = pl.ds(THIRDS + 4 * r, 4)
        return pltpu.make_async_copy(held.at[at, h], out_ref.at[at, h], out_sem.at[r, h])

    def absorb(r, h):
        parity = r % 2
        for k in range(4):
            remote(parity, h, k).wait_recv()

        def work(at):
            for k in range(4):
                held[THIRDS + 4 * r + k, h, at, :] = land[parity, h, k, at, :]

        each_chunk(work)
        keep(r, h).start()

    def send(r, h):
        parity = r % 2
        source = [table_ref[targets[k], 4 * r + k] for k in range(4)]

        def work(at):
            for k in range(4):
                stage[parity, h, k, at, :] = held[source[k], h, at, :]

        each_chunk(work)
        for k in range(4):
            remote(parity, h, k).start()

    dims = (((1,), (1,)), ((), ()))
    quads = spread.shape[2] // QUAD

    def begin(h):
        stay(h).wait()
        for i in range(1, bands):
            from_band(h, i).wait_recv()
        if h + LEAD < STREAMS:
            spread_out(h + LEAD)

        def turn(g, carry):
            s, part = g // quads, g % quads
            wide = jnp.concatenate([spread[h, s, part * QUAD + q] for q in range(QUAD)], axis=1)
            value = lax.dot_general(pick_ref[...], wide, dims, preferred_element_type=jnp.float32)
            at = pl.ds(pl.multiple_of(part * (QUAD * KROWS), QUAD * KROWS), QUAD * KROWS)
            held[s, h, at, :] = value.astype(jnp.bfloat16)
            return carry

        lax.fori_loop(0, THIRDS * quads, turn, 0)
        send(0, h)
        keep_own(h).start()

    def free(parity, h):
        for k in range(4):
            remote(parity, h, k).wait_send()

    def advance(r, h):
        absorb(r - 1, h)
        free(r % 2, h)
        send(r, h)

    def second(h):
        absorb(0, h)
        send(1, h)

    for h in range(LEAD):
        spread_out(h)
    peeled = max(DELAYS) + 2
    for t in range(peeled):
        for h in range(STREAMS):
            if t - DELAYS[h] == 0:
                begin(h)
            elif t - DELAYS[h] == 1:
                second(h)
            elif t - DELAYS[h] > 1:
                advance(t - DELAYS[h], h)

    def general(t, carry):
        for h in range(STREAMS):
            advance(t - DELAYS[h], h)
        return carry

    lax.fori_loop(peeled, rounds, general, 0)
    for t in range(rounds, rounds + max(DELAYS) + 1):
        for h in range(STREAMS):
            if t - DELAYS[h] == rounds:
                absorb(rounds - 1, h)
            elif t - DELAYS[h] < rounds:
                advance(t - DELAYS[h], h)
    for h in range(STREAMS):
        for parity in range(2):
            free(parity, h)
        for i in range(1, bands):
            to_band(h, i).wait_send()
        keep_own(h).wait()
        for r in range(rounds):
            keep(r, h).wait()


def exchange(table, white, count, rounds, ident):
    bands, _, _, freqs, sub, _ = white.shape
    rows = freqs * KROWS
    block = bands * sub
    shape = (THIRDS + 4 * rounds, STREAMS, rows, block)
    any_space = pl.BlockSpec(memory_space=pl.ANY)
    return pl.pallas_call(
        functools.partial(exchange_kernel, count, bands, rounds),
        out_shape=jax.ShapeDtypeStruct(shape, white.dtype),
        in_specs=[
            pl.BlockSpec(memory_space=pltpu.SMEM),
            any_space,
            pl.BlockSpec(memory_space=pltpu.VMEM),
        ],
        out_specs=any_space,
        scratch_shapes=[
            pltpu.VMEM(shape, white.dtype),
            pltpu.VMEM((STREAMS, THIRDS, freqs, block, LANES), white.dtype),
            pltpu.VMEM((2, STREAMS, 4, rows, block), white.dtype),
            pltpu.VMEM((2, STREAMS, 4, rows, block), white.dtype),
            pltpu.SemaphoreType.DMA((2, STREAMS, 4)),
            pltpu.SemaphoreType.DMA((2, STREAMS, 4)),
            pltpu.SemaphoreType.DMA((rounds + 1, STREAMS)),
            pltpu.SemaphoreType.DMA((STREAMS, bands)),
            pltpu.SemaphoreType.DMA((STREAMS, bands)),
            pltpu.SemaphoreType.DMA((STREAMS,)),
        ],
        compiler_params=pltpu.CompilerParams(
            vmem_limit_bytes=EXCHANGE_LIMIT, collective_id=ident, has_side_effects=True
        ),
    )(table, white, jnp.asarray(pick_table()))


def gather_all(white):
    bands, _, _, freqs, sub, _ = white.shape
    banded = white.reshape(bands, THIRDS * STREAMS * freqs, sub, LANES)
    banded = lax.all_to_all(banded, "tm", split_axis=0, concat_axis=0, tiled=True)
    own = compact(banded).reshape(THIRDS, STREAMS, freqs * KROWS, bands * sub)
    count = lax.axis_size("chan")
    copies = jnp.broadcast_to(own[None], (count,) + own.shape)
    copies = lax.all_to_all(copies, "chan", split_axis=0, concat_axis=0, tiled=True)
    return copies.reshape((count * THIRDS,) + own.shape[1:])


def cross_spectra(table, slot_of, rounds, white, blocks, live, count):
    thirds = jnp.arange(THIRDS, dtype=jnp.int32)[None, :]
    chosen = slot_of[blocks[:, None] + count * thirds]
    everywhere = blocks[:, None] * THIRDS + thirds
    chosen, everywhere, live, white = lax.optimization_barrier((chosen, everywhere, live, white))

    def by_rounds(choice, ident):
        def run():
            held = exchange(table, white, count, choice, ident)
            return products(held, chosen, live)

        return run

    def whole():
        return products(gather_all(white), everywhere, live)

    branches = [by_rounds(choice, i) for i, choice in enumerate(ROUND_CHOICES)] + [whole]
    which = sum((rounds > choice).astype(jnp.int32) for choice in ROUND_CHOICES)
    return lax.switch(which, branches)


def product_kernel(needed_ref, live_ref, left_ref, right_ref, out_ref):
    slot = pl.program_id(0)
    streams, rows, block = left_ref.shape[1:]
    norm = 1.0 / math.sqrt(SEG)
    dims = (((0,), (0,)), ((), ()))
    per = rows // (QUAD * KROWS)

    @pl.when(live_ref[slot] != 0)
    def _():
        def one(g, carry):
            at = pl.ds(pl.multiple_of(g % per * (QUAD * KROWS), 16), QUAD * KROWS)
            left4 = left_ref[0, g // per, at]
            right4 = right_ref[0, g // per, at]
            for q in range(QUAD):
                left = left4[q * KROWS : (q + 1) * KROWS]
                right = right4[q * KROWS : (q + 1) * KROWS]
                turned = jnp.concatenate([-right[SEG:], right[:SEG]], axis=0)
                both = jnp.concatenate([right, turned], axis=1)
                value = lax.dot_general(left, both, dims, preferred_element_type=jnp.float32)
                value = (value * norm).astype(jnp.bfloat16)
                out_ref[0, g * QUAD + q, 0] = value[:, :block]
                out_ref[0, g * QUAD + q, 1] = value[:, block:]
            return carry

        lax.fori_loop(0, streams * per, one, 0, unroll=True)

    @pl.when(live_ref[slot] == 0)
    def _():
        out_ref[...] = jnp.zeros_like(out_ref)


def products(held, needed, live):
    _, streams, rows, block = held.shape
    part = streams * (rows // KROWS)
    spec = (1, streams, rows, block)
    return pl.pallas_call(
        product_kernel,
        out_shape=jax.ShapeDtypeStruct((PMAX, THIRDS * part, 2, block, block), jnp.bfloat16),
        grid_spec=pltpu.PrefetchScalarGridSpec(
            num_scalar_prefetch=2,
            grid=(PMAX, THIRDS),
            in_specs=[
                pl.BlockSpec(spec, lambda s, g, need, live: (need[2 * s, g], 0, 0, 0)),
                pl.BlockSpec(spec, lambda s, g, need, live: (need[2 * s + 1, g], 0, 0, 0)),
            ],
            out_specs=pl.BlockSpec((1, part, 2, block, block), lambda s, g, need, live: (s, g, 0, 0, 0)),
        ),
        compiler_params=pltpu.CompilerParams(vmem_limit_bytes=PRODUCT_LIMIT),
    )(needed, live, held, held)


def body(records, pairs, owners, starts):
    tm_count = lax.axis_size("tm")
    chan_count = lax.axis_size("chan")
    chans, samp_dev = records.shape
    block = chans // chan_count
    sub = block // tm_count
    group_freq = NFREQ // tm_count
    table, slots, rounds = plan(pairs, owners, chan_count)
    moved = (records * SCALE).astype(jnp.float16).reshape(chan_count * tm_count, sub, samp_dev)
    received = lax.all_to_all(moved, ("chan", "tm"), split_axis=0, concat_axis=0, tiled=True)
    white = spectra(starts, received.astype(jnp.float32), chan_count, tm_count)
    white = white.reshape(tm_count, THIRDS, STREAMS, group_freq // (THIRDS * STREAMS), sub, LANES)
    me_chan = lax.axis_index("chan")
    pair_id, live = slot_table(owners, chan_count)
    mine = lax.dynamic_slice_in_dim(pair_id, me_chan * PMAX, PMAX)
    my_live = lax.dynamic_slice_in_dim(live, me_chan * PMAX, PMAX).astype(jnp.int32)
    blocks = pairs[mine].reshape(2 * PMAX)
    slot_of = lax.dynamic_index_in_dim(slots, me_chan, 0, keepdims=False)
    return cross_spectra(table, slot_of, rounds[0, 0], white, blocks, my_live, chan_count)


def solution(mesh):
    return jax.shard_map(
        body,
        mesh=mesh,
        in_specs=(P(None, ("tm", "chan")), P(), P(), P()),
        out_specs=P("chan", "tm", None, None, None),
        check_vma=False,
    )
```

```python
import functools
import math
import jax
import jax.numpy as jnp
import ml_dtypes
import numpy as np
from jax import lax
from jax.experimental import pallas as pl
from jax.experimental.pallas import tpu as pltpu
from jax.sharding import PartitionSpec as P

NFFT = 1024
NFREQ = 384
WBAND = 64
SEG = 58
SEGP = 64
PMAX = 6
LANES = 128
KROWS = 2 * SEG
QUAD = 4
VMEM_LIMIT = 56 * 1024 * 1024
EXCHANGE_LIMIT = 28 * 1024 * 1024
PRODUCT_LIMIT = 16 * 1024 * 1024
THIRDS = 3
STREAMS = 4
DELAYS = (0, 0, 1, 1)
LEAD = 2
MAX_ROUNDS = 32
ROUND_CHOICES = (7, 8, 9)
RULES = (3, 7)
SCALE = 8192.0


def windowed_table():
    sample = np.arange(NFFT)
    freq = np.arange(NFREQ)
    angle = 2.0 * np.pi * ((freq[:, None] * sample[None, :]) % NFFT) / NFFT
    window = 0.5 - 0.5 * np.cos(2.0 * np.pi * sample / NFFT)
    table = np.concatenate([np.cos(angle), -np.sin(angle)], axis=0) * window[None, :] / SCALE
    high = table.astype(np.float32).astype(ml_dtypes.bfloat16)
    low = (table - high.astype(np.float64)).astype(np.float32).astype(ml_dtypes.bfloat16)
    return high, low


def pick_table():
    pick = np.zeros((QUAD * KROWS, QUAD * LANES), np.float32)
    for q in range(QUAD):
        for part in range(2):
            for s in range(SEG):
                pick[q * KROWS + part * SEG + s, q * LANES + part * SEGP + s] = 1.0
    return pick.astype(ml_dtypes.bfloat16)


def slot_table(owners, owner_count):
    owner = owners[:, 0]
    npair = owner.shape[0]
    order = jnp.arange(npair, dtype=jnp.int32)
    same = owner[:, None] == owner[None, :]
    before = order[None, :] < order[:, None]
    rank = jnp.sum((same & before).astype(jnp.int32), axis=1)
    target = owner * PMAX + rank
    rows = jnp.arange(owner_count * PMAX, dtype=jnp.int32)
    match = target[None, :] == rows[:, None]
    live = jnp.any(match, axis=1)
    pair_id = jnp.sum(jnp.where(match, order[None, :], 0), axis=1)
    return (pair_id, live)


def bits(size):
    assert size & (size - 1) == 0
    return size.bit_length() - 1


def spectra_kernel(
    chan_count, tm_count, starts_ref, rec_ref, high_hbm, low_hbm, out_ref, high_ref, low_ref, frames, spread, sems
):
    fetch = [
        pltpu.make_async_copy(high_hbm, high_ref, sems.at[0]),
        pltpu.make_async_copy(low_hbm, low_ref, sems.at[1]),
    ]
    for copy in fetch:
        copy.start()
    sub = rec_ref.shape[1]
    tiles = rec_ref.shape[2] // LANES
    total_tiles = rec_ref.shape[0] * tiles
    width = NFFT // LANES
    lane = lax.broadcasted_iota(jnp.int32, (sub, LANES), 1)
    for c in range(sub):
        frames[:, c * SEGP + SEG : (c + 1) * SEGP, :] = jnp.zeros(
            (width, SEGP - SEG, LANES), jnp.float32
        )

    def cut(s, carry):
        begin = starts_ref[s]
        base = jnp.minimum(begin >> bits(LANES), total_tiles - width - 1)
        over = begin - base * LANES
        shift = (LANES - over) & (LANES - 1)
        turned = []
        for j in range(width + 1):
            tile = base + j
            piece = tile >> bits(tiles)
            source = (piece & (chan_count - 1)) * tm_count + (piece >> bits(chan_count))
            at = pl.multiple_of((tile & (tiles - 1)) * LANES, LANES)
            turned.append(pltpu.roll(rec_ref[source, :, pl.ds(at, LANES)], shift, 1))
        keep = lane < LANES - over
        for j in range(width):
            frames[j, pl.ds(s, sub, stride=SEGP), :] = jnp.where(keep, turned[j], turned[j + 1])
        return carry

    lax.fori_loop(0, SEG // 4 * 4, cut, 0, unroll=4)
    for s in range(SEG // 4 * 4, SEG):
        cut(s, 0)
    for copy in fetch:
        copy.wait()

    group = 4
    cols = group * SEGP
    dims = (((1,), (1,)), ((), ()))
    half = lax.broadcasted_iota(jnp.int32, (NFREQ, LANES), 1) < SEGP

    def transform(g, carry):
        at = pl.ds(pl.multiple_of(g * cols, cols), cols)
        rows = jnp.concatenate([frames[j, at, :] for j in range(width)], axis=1)
        top = rows.astype(jnp.bfloat16)
        rest = (rows - top.astype(jnp.float32)).astype(jnp.bfloat16)
        parts = []
        for p in range(2):
            hi = high_ref[p * NFREQ : (p + 1) * NFREQ, :]
            lo = low_ref[p * NFREQ : (p + 1) * NFREQ, :]
            value = lax.dot_general(hi, rest, dims, preferred_element_type=jnp.float32)
            value += lax.dot_general(lo, top, dims, preferred_element_type=jnp.float32)
            value += lax.dot_general(hi, top, dims, preferred_element_type=jnp.float32)
            parts.append(value)
        re, im = parts
        power = re * re + im * im
        band = jnp.mean(power.reshape(NFREQ // WBAND, WBAND, cols), axis=1, keepdims=True)
        scale = 1.0 / jnp.sqrt(band + 1e-06)
        scale = jnp.broadcast_to(scale, (NFREQ // WBAND, WBAND, cols)).reshape(NFREQ, cols)
        re = re * scale
        im = im * scale
        for h in range(group // 2):
            a = re[:, h * LANES : (h + 1) * LANES]
            b = im[:, h * LANES : (h + 1) * LANES]
            c = g * group + 2 * h
            even = pl.multiple_of(c * NFREQ, NFREQ)
            spread[pl.ds(even, NFREQ), :] = jnp.where(half, a, pltpu.roll(b, SEGP, 1))
            odd = pl.multiple_of((c + 1) * NFREQ, NFREQ)
            spread[pl.ds(odd, NFREQ), :] = jnp.where(half, pltpu.roll(a, SEGP, 1), b)
        return carry

    lax.fori_loop(0, sub // group, transform, 0, unroll=2)

    def regroup(f, carry):
        for u in range(8):
            k = f * 8 + u
            out_ref[k] = spread[pl.ds(k, sub, stride=NFREQ), :].astype(jnp.bfloat16)
        return carry

    lax.fori_loop(0, NFREQ // 8, regroup, 0, unroll=4)


def spectra(starts, received, chan_count, tm_count):
    sub = received.shape[1]
    high, low = windowed_table()
    vmem = pl.BlockSpec(memory_space=pltpu.VMEM)
    return pl.pallas_call(
        functools.partial(spectra_kernel, chan_count, tm_count),
        out_shape=jax.ShapeDtypeStruct((NFREQ, sub, LANES), jnp.bfloat16),
        in_specs=[
            pl.BlockSpec(memory_space=pltpu.SMEM),
            vmem,
            pl.BlockSpec(memory_space=pl.ANY),
            pl.BlockSpec(memory_space=pl.ANY),
        ],
        out_specs=vmem,
        scratch_shapes=[
            pltpu.VMEM(high.shape, high.dtype),
            pltpu.VMEM(low.shape, low.dtype),
            pltpu.VMEM((NFFT // LANES, sub * SEGP, LANES), jnp.float32),
            pltpu.VMEM((sub * NFREQ, LANES), jnp.float32),
            pltpu.SemaphoreType.DMA((2,)),
        ],
        compiler_params=pltpu.CompilerParams(vmem_limit_bytes=VMEM_LIMIT),
    )(starts, received, jnp.asarray(high), jnp.asarray(low))


def compact_kernel(in_ref, pick_ref, out_ref):
    pieces, freqs, sub, _ = in_ref.shape
    block = pieces * sub
    dims = (((1,), (1,)), ((), ()))

    def one(g, carry):
        wide = jnp.concatenate(
            [
                jnp.concatenate([in_ref[p, g * QUAD + q] for p in range(pieces)], axis=0)
                for q in range(QUAD)
            ],
            axis=1,
        )
        value = lax.dot_general(pick_ref[...], wide, dims, preferred_element_type=jnp.float32)
        out_ref[g] = value.astype(jnp.bfloat16)
        return carry

    lax.fori_loop(0, freqs // QUAD, one, 0)


def compact(banded):
    pieces, freqs, sub, _ = banded.shape
    vmem = pl.BlockSpec(memory_space=pltpu.VMEM)
    return pl.pallas_call(
        compact_kernel,
        out_shape=jax.ShapeDtypeStruct((freqs // QUAD, QUAD * KROWS, pieces * sub), jnp.bfloat16),
        in_specs=[vmem, vmem],
        out_specs=vmem,
        compiler_params=pltpu.CompilerParams(vmem_limit_bytes=VMEM_LIMIT),
    )(banded, jnp.asarray(pick_table()))


def torus_tables(count):
    side = math.isqrt(count)
    index = np.arange(count)
    x, y = index // side, index % side
    sources = [
        (x + 1) % side * side + y,
        (x - 1) % side * side + y,
        x * side + (y + 1) % side,
        x * side + (y - 1) % side,
    ]
    every = np.eye(len(RULES))
    near = np.concatenate([np.kron(every, np.eye(count)[source]) for source in sources], axis=0)
    dx = np.abs(x[:, None] - x[None, :])
    dy = np.abs(y[:, None] - y[None, :])
    dist = np.minimum(dx, side - dx) + np.minimum(dy, side - dy)
    reach = np.concatenate([np.kron(every, dist <= d) for d in range(4)], axis=0)
    shell = np.concatenate([np.kron(every, (dist == d) * 2.0 ** (3 - d)) for d in range(4)], axis=1)
    return [t.astype(ml_dtypes.bfloat16) for t in (near, reach, shell)]


def plan_kernel(pairs_ref, owners_ref, near_ref, reach_ref, shell_ref, table_ref, slots_ref, rounds_ref):
    rows = near_ref.shape[1]
    count = rows // len(RULES)
    shape = (rows, LANES)
    row = lax.broadcasted_iota(jnp.int32, shape, 0)
    node = row % count
    turn = jnp.where(row < count, RULES[0], RULES[1])
    lane = lax.broadcasted_iota(jnp.int32, shape, 1)
    inside = lane < THIRDS * count
    block = lane % count
    third = lane // count
    commodities = THIRDS * count
    tie = commodities - 1 - (lane + turn * node) % commodities
    tie = jnp.where(inside, tie, 0).astype(jnp.float32)

    def mark(p, need):
        hit = (block == pairs_ref[p, 0]) | (block == pairs_ref[p, 1])
        return jnp.where(hit & (node == owners_ref[p, 0]) & inside, 1.0, need)

    need = lax.fori_loop(0, pairs_ref.shape[0], mark, jnp.zeros(shape, jnp.float32))
    has = jnp.where((block == node) & inside, 1.0, 0.0)
    slot_of = jnp.where(has > 0, third, 0).astype(jnp.float32)
    table = jnp.zeros(shape, jnp.float32)

    def dot(m, v):
        return jnp.dot(m, v.astype(jnp.bfloat16), preferred_element_type=jnp.float32)

    def unfinished(state):
        r, left, _, _, _ = state
        return (left > 0) & (r < MAX_ROUNDS)

    def one(state):
        r, _, has, slot_of, table = state
        rem = need * (1.0 - has)
        short = rem * jnp.sum(rem, axis=1, keepdims=True)
        reached = dot(reach_ref[...], has)
        waves = jnp.concatenate(
            [jnp.where(reached[d * rows : (d + 1) * rows] > 0, 0.0, short) for d in range(4)], axis=0
        )
        gain = dot(shell_ref[...], waves)
        both = dot(near_ref[...], jnp.concatenate([has, slot_of], axis=1))
        near_has = [both[k * rows : (k + 1) * rows, :LANES] for k in range(4)]
        near_slot = [both[k * rows : (k + 1) * rows, LANES:] for k in range(4)]
        sources = near_has[0] + near_has[1] + near_has[2] + near_has[3]
        scarce = 5.0 - sources
        worth = jnp.where((gain > 0) & (has == 0), gain * scarce * scarce * 64.0 + tie, 0.0)
        for k in range(4):
            key = worth * near_has[k]
            best = jnp.max(key, axis=1, keepdims=True)
            chosen = (key == best) & (key > 0)
            worth = jnp.where(chosen, 0.0, worth)
            has = jnp.where(chosen, 1.0, has)
            source = jnp.sum(jnp.where(chosen, near_slot[k], 0.0), axis=1, keepdims=True)
            table = jnp.where(lane == 4 * r + k, source, table)
            slot_of = jnp.where(chosen, (THIRDS + 4 * r + k).astype(jnp.float32), slot_of)
        return r + 1, jnp.minimum(*missing(has)), has, slot_of, table

    def missing(has):
        rem = need * (1.0 - has)
        return jnp.sum(rem[:count]), jnp.sum(rem[count:])

    rounds, left, has, slot_of, table = lax.while_loop(
        unfinished, one, (jnp.int32(0), jnp.float32(1.0), has, slot_of, table)
    )
    first = missing(has)[0] == 0
    table_ref[...] = jnp.where(first, table[:count], table[count:]).astype(jnp.int32)
    slots_ref[...] = jnp.where(first, slot_of[:count], slot_of[count:]).astype(jnp.int32)
    rounds_ref[...] = jnp.full(rounds_ref.shape, jnp.where(left > 0, MAX_ROUNDS, rounds), jnp.int32)


def plan(pairs, owners, count):
    near, reach, shell = torus_tables(count)
    vmem = pl.BlockSpec(memory_space=pltpu.VMEM)
    smem = pl.BlockSpec(memory_space=pltpu.SMEM)
    grid = jax.ShapeDtypeStruct((count, LANES), jnp.int32)
    return pl.pallas_call(
        plan_kernel,
        out_shape=(grid, grid, jax.ShapeDtypeStruct((8, LANES), jnp.int32)),
        in_specs=[smem, smem, vmem, vmem, vmem],
        out_specs=(vmem, vmem, vmem),
    )(pairs, owners, jnp.asarray(near), jnp.asarray(reach), jnp.asarray(shell))


def exchange_kernel(
    count,
    bands,
    rounds,
    table_ref,
    white_ref,
    pick_ref,
    out_ref,
    held,
    spread,
    land,
    stage,
    send_sem,
    recv_sem,
    out_sem,
    band_send,
    band_recv,
    band_own,
):
    side = math.isqrt(count)
    me = lax.axis_index("chan")
    x, y = me // side, me % side
    targets = [
        (x + side - 1) % side * side + y,
        (x + 1) % side * side + y,
        x * side + (y + side - 1) % side,
        x * side + (y + 1) % side,
    ]
    rows = held.shape[2]
    sub = white_ref.shape[4]
    step = 16
    band = lax.axis_index("tm")

    barrier = pltpu.get_barrier_semaphore()
    for k in range(4):
        pl.semaphore_signal(
            barrier, inc=1, device_id={"chan": targets[k]}, device_id_type=pl.DeviceIdType.MESH
        )
    for i in range(1, bands):
        pl.semaphore_signal(
            barrier, inc=1, device_id={"tm": (band + i) % bands}, device_id_type=pl.DeviceIdType.MESH
        )
    pl.semaphore_wait(barrier, 4 + bands - 1)

    def place(source):
        return pl.ds(pl.multiple_of(source * sub, sub), sub)

    def band_copy(h, i, source, target, peer):
        return pltpu.make_async_remote_copy(
            src_ref=white_ref.at[target, :, h],
            dst_ref=spread.at[h, :, :, place(source)],
            send_sem=band_send.at[h, i],
            recv_sem=band_recv.at[h, i],
            device_id={"tm": peer},
            device_id_type=pl.DeviceIdType.MESH,
        )

    def to_band(h, i):
        target = (band + i) % bands
        return band_copy(h, i, band, target, target)

    def from_band(h, i):
        source = (band + bands - i) % bands
        return band_copy(h, i, source, source, source)

    def stay(h):
        return pltpu.make_async_copy(
            white_ref.at[band, :, h], spread.at[h, :, :, place(band)], band_own.at[h]
        )

    def spread_out(h):
        for i in range(1, bands):
            to_band(h, i).start()
        stay(h).start()

    def each_chunk(work):
        def run(i, carry):
            work(pl.ds(pl.multiple_of(i * step, step), step))
            return carry

        lax.fori_loop(0, rows // step, run, 0)

    def remote(parity, h, k):
        return pltpu.make_async_remote_copy(
            src_ref=stage.at[parity, h, k],
            dst_ref=land.at[parity, h, k],
            send_sem=send_sem.at[parity, h, k],
            recv_sem=recv_sem.at[parity, h, k],
            device_id={"chan": targets[k]},
            device_id_type=pl.DeviceIdType.MESH,
        )

    def keep_own(h):
        return pltpu.make_async_copy(
            held.at[pl.ds(0, THIRDS), h], out_ref.at[pl.ds(0, THIRDS), h], out_sem.at[rounds, h]
        )

    def keep(r, h):
        at = pl.ds(THIRDS + 4 * r, 4)
        return pltpu.make_async_copy(held.at[at, h], out_ref.at[at, h], out_sem.at[r, h])

    def absorb(r, h):
        parity = r % 2
        for k in range(4):
            remote(parity, h, k).wait_recv()

        def work(at):
            for k in range(4):
                held[THIRDS + 4 * r + k, h, at, :] = land[parity, h, k, at, :]

        each_chunk(work)
        keep(r, h).start()

    def send(r, h):
        parity = r % 2
        source = [table_ref[targets[k], 4 * r + k] for k in range(4)]

        def work(at):
            for k in range(4):
                stage[parity, h, k, at, :] = held[source[k], h, at, :]

        each_chunk(work)
        for k in range(4):
            remote(parity, h, k).start()

    dims = (((1,), (1,)), ((), ()))
    quads = spread.shape[2] // QUAD

    def begin(h):
        stay(h).wait()
        for i in range(1, bands):
            from_band(h, i).wait_recv()
        if h + LEAD < STREAMS:
            spread_out(h + LEAD)

        def turn(g, carry):
            s, part = g // quads, g % quads
            wide = jnp.concatenate([spread[h, s, part * QUAD + q] for q in range(QUAD)], axis=1)
            value = lax.dot_general(pick_ref[...], wide, dims, preferred_element_type=jnp.float32)
            at = pl.ds(pl.multiple_of(part * (QUAD * KROWS), QUAD * KROWS), QUAD * KROWS)
            held[s, h, at, :] = value.astype(jnp.bfloat16)
            return carry

        lax.fori_loop(0, THIRDS * quads, turn, 0)
        send(0, h)
        keep_own(h).start()

    def free(parity, h):
        for k in range(4):
            remote(parity, h, k).wait_send()

    def advance(r, h):
        absorb(r - 1, h)
        free(r % 2, h)
        send(r, h)

    def second(h):
        absorb(0, h)
        send(1, h)

    for h in range(LEAD):
        spread_out(h)
    peeled = max(DELAYS) + 2
    for t in range(peeled):
        for h in range(STREAMS):
            if t - DELAYS[h] == 0:
                begin(h)
            elif t - DELAYS[h] == 1:
                second(h)
            elif t - DELAYS[h] > 1:
                advance(t - DELAYS[h], h)

    def general(t, carry):
        for h in range(STREAMS):
            advance(t - DELAYS[h], h)
        return carry

    lax.fori_loop(peeled, rounds, general, 0)
    for t in range(rounds, rounds + max(DELAYS) + 1):
        for h in range(STREAMS):
            if t - DELAYS[h] == rounds:
                absorb(rounds - 1, h)
            elif t - DELAYS[h] < rounds:
                advance(t - DELAYS[h], h)
    for h in range(STREAMS):
        for parity in range(2):
            free(parity, h)
        for i in range(1, bands):
            to_band(h, i).wait_send()
        keep_own(h).wait()
        for r in range(rounds):
            keep(r, h).wait()


def exchange(table, white, count, rounds, ident):
    bands, _, _, freqs, sub, _ = white.shape
    rows = freqs * KROWS
    block = bands * sub
    shape = (THIRDS + 4 * rounds, STREAMS, rows, block)
    any_space = pl.BlockSpec(memory_space=pl.ANY)
    return pl.pallas_call(
        functools.partial(exchange_kernel, count, bands, rounds),
        out_shape=jax.ShapeDtypeStruct(shape, white.dtype),
        in_specs=[
            pl.BlockSpec(memory_space=pltpu.SMEM),
            any_space,
            pl.BlockSpec(memory_space=pltpu.VMEM),
        ],
        out_specs=any_space,
        scratch_shapes=[
            pltpu.VMEM(shape, white.dtype),
            pltpu.VMEM((STREAMS, THIRDS, freqs, block, LANES), white.dtype),
            pltpu.VMEM((2, STREAMS, 4, rows, block), white.dtype),
            pltpu.VMEM((2, STREAMS, 4, rows, block), white.dtype),
            pltpu.SemaphoreType.DMA((2, STREAMS, 4)),
            pltpu.SemaphoreType.DMA((2, STREAMS, 4)),
            pltpu.SemaphoreType.DMA((rounds + 1, STREAMS)),
            pltpu.SemaphoreType.DMA((STREAMS, bands)),
            pltpu.SemaphoreType.DMA((STREAMS, bands)),
            pltpu.SemaphoreType.DMA((STREAMS,)),
        ],
        compiler_params=pltpu.CompilerParams(
            vmem_limit_bytes=EXCHANGE_LIMIT, collective_id=ident, has_side_effects=True
        ),
    )(table, white, jnp.asarray(pick_table()))


def gather_all(white):
    bands, _, _, freqs, sub, _ = white.shape
    banded = white.reshape(bands, THIRDS * STREAMS * freqs, sub, LANES)
    banded = lax.all_to_all(banded, "tm", split_axis=0, concat_axis=0, tiled=True)
    own = compact(banded).reshape(THIRDS, STREAMS, freqs * KROWS, bands * sub)
    count = lax.axis_size("chan")
    copies = jnp.broadcast_to(own[None], (count,) + own.shape)
    copies = lax.all_to_all(copies, "chan", split_axis=0, concat_axis=0, tiled=True)
    return copies.reshape((count * THIRDS,) + own.shape[1:])


def cross_spectra(table, slot_of, rounds, white, blocks, live, count):
    thirds = jnp.arange(THIRDS, dtype=jnp.int32)[None, :]
    chosen = slot_of[blocks[:, None] + count * thirds]
    everywhere = blocks[:, None] * THIRDS + thirds
    chosen, everywhere, live, white = lax.optimization_barrier((chosen, everywhere, live, white))

    def by_rounds(choice, ident):
        def run():
            held = exchange(table, white, count, choice, ident)
            return products(held, chosen, live)

        return run

    def whole():
        return products(gather_all(white), everywhere, live)

    branches = [by_rounds(choice, i) for i, choice in enumerate(ROUND_CHOICES)] + [whole]
    which = sum((rounds > choice).astype(jnp.int32) for choice in ROUND_CHOICES)
    return lax.switch(which, branches)


def product_kernel(needed_ref, live_ref, *refs):
    slot = pl.program_id(0)
    lefts, rights, out_ref = refs[:THIRDS], refs[THIRDS : 2 * THIRDS], refs[-1]
    streams, rows, block = lefts[0].shape[1:]
    norm = 1.0 / math.sqrt(SEG)
    dims = (((0,), (0,)), ((), ()))
    per = rows // (QUAD * KROWS)
    quads = streams * per

    @pl.when(live_ref[slot] != 0)
    def _():
        for s in range(THIRDS):

            def one(g, carry):
                at = pl.ds(pl.multiple_of(g % per * (QUAD * KROWS), 16), QUAD * KROWS)
                left4 = lefts[s][0, g // per, at]
                right4 = rights[s][0, g // per, at]
                for q in range(QUAD):
                    left = left4[q * KROWS : (q + 1) * KROWS]
                    right = right4[q * KROWS : (q + 1) * KROWS]
                    turned = jnp.concatenate([-right[SEG:], right[:SEG]], axis=0)
                    both = jnp.concatenate([right, turned], axis=1)
                    value = lax.dot_general(left, both, dims, preferred_element_type=jnp.float32)
                    value = (value * norm).astype(jnp.bfloat16)
                    out_ref[0, (s * quads + g) * QUAD + q, 0] = value[:, :block]
                    out_ref[0, (s * quads + g) * QUAD + q, 1] = value[:, block:]
                return carry

            lax.fori_loop(0, quads, one, 0, unroll=True)

    @pl.when(live_ref[slot] == 0)
    def _():
        out_ref[...] = jnp.zeros_like(out_ref)


def products(held, needed, live):
    _, streams, rows, block = held.shape
    freqs = THIRDS * streams * (rows // KROWS)
    spec = (1, streams, rows, block)

    def take(side, third):
        return pl.BlockSpec(spec, lambda s, need, live: (need[2 * s + side, third], 0, 0, 0))

    return pl.pallas_call(
        product_kernel,
        out_shape=jax.ShapeDtypeStruct((PMAX, freqs, 2, block, block), jnp.bfloat16),
        grid_spec=pltpu.PrefetchScalarGridSpec(
            num_scalar_prefetch=2,
            grid=(PMAX,),
            in_specs=[take(side, third) for side in range(2) for third in range(THIRDS)],
            out_specs=pl.BlockSpec((1, freqs, 2, block, block), lambda s, need, live: (s, 0, 0, 0, 0)),
        ),
        compiler_params=pltpu.CompilerParams(vmem_limit_bytes=PRODUCT_LIMIT),
    )(needed, live, *[held] * (2 * THIRDS))


def body(records, pairs, owners, starts):
    tm_count = lax.axis_size("tm")
    chan_count = lax.axis_size("chan")
    chans, samp_dev = records.shape
    block = chans // chan_count
    sub = block // tm_count
    group_freq = NFREQ // tm_count
    table, slots, rounds = plan(pairs, owners, chan_count)
    moved = (records * SCALE).astype(jnp.float16).reshape(chan_count * tm_count, sub, samp_dev)
    received = lax.all_to_all(moved, ("chan", "tm"), split_axis=0, concat_axis=0, tiled=True)
    white = spectra(starts, received.astype(jnp.float32), chan_count, tm_count)
    white = white.reshape(tm_count, THIRDS, STREAMS, group_freq // (THIRDS * STREAMS), sub, LANES)
    me_chan = lax.axis_index("chan")
    pair_id, live = slot_table(owners, chan_count)
    mine = lax.dynamic_slice_in_dim(pair_id, me_chan * PMAX, PMAX)
    my_live = lax.dynamic_slice_in_dim(live, me_chan * PMAX, PMAX).astype(jnp.int32)
    blocks = pairs[mine].reshape(2 * PMAX)
    slot_of = lax.dynamic_index_in_dim(slots, me_chan, 0, keepdims=False)
    return cross_spectra(table, slot_of, rounds[0, 0], white, blocks, my_live, chan_count)


def solution(mesh):
    return jax.shard_map(
        body,
        mesh=mesh,
        in_specs=(P(None, ("tm", "chan")), P(), P(), P()),
        out_specs=P("chan", "tm", None, None, None),
        check_vma=False,
    )
```
